128 devices in a mesh: ctx: 64 (over z, x, y_hi, core), head: 2 (over y_lo).
Axes of the slice: x: 4, y: 4 (y_hi: 2, y_lo: 2; y = y_hi * 2 + y_lo), z: 4, core: 2. Of those that a mesh axis runs over, the one named last changes fastest.
Arguments:
- queries: bfloat16 [24576, 4096], P(('ctx', 'head')), may hold values from -6 to 6
- keys: bfloat16 [24576, 4096], P(('ctx', 'head')), may hold values from -6 to 6
- values: bfloat16 [24576, 4096], P(('ctx', 'head')), may hold values from -6 to 6
- grad_out: bfloat16 [24576, 4096], P(('ctx', 'head')), may hold values from -6 to 6
- pattern: int32 [64, 4], P('ctx'), may hold values 0 or 1
- phase: int32 [64, 4], P('ctx'), may hold values from 0 to 7
Outputs:
- grad_queries: bfloat16 [24576, 4096], P(('ctx', 'head'))
- grad_keys: bfloat16 [24576, 4096], P(('ctx', 'head'))
- grad_values: bfloat16 [24576, 4096], P(('ctx', 'head'))
The draws below stay inside these ranges and needn't reach their ends.
All inputs are finite; a program needn't handle non-finite values. No bound on the sum of `pattern` on one device may be relied on, other than what follows from the above.
Results may differ from the reference program's by a relative error of at most 0.04.
Values may be sent and summed in bfloat16 or wider, within the bound.
No kernel may reach another device: no remote copies, remote signals or barrier semaphores. Data moves between devices by JAX's collectives and lax.ppermute only.
A program may use at most 192 MiB of HBM per device.

```python
import jax
import jax.numpy as jnp
from jax import lax

HEADS = 32
HD = 128
BLK = 384
LEVELS = 4
NBLOCKS = 64
TOKENS = 24576


def draw_queries(key, part):
    key = jax.random.fold_in(key, 11)
    return jnp.clip(jax.random.normal(key, (TOKENS, HEADS * HD)), -4.0, 4.0).astype(jnp.bfloat16)


def draw_keys(key, part):
    key = jax.random.fold_in(key, 23)
    return jnp.clip(jax.random.normal(key, (TOKENS, HEADS * HD)), -4.0, 4.0).astype(jnp.bfloat16)


def place_ends(drawn, stream_key, smallest, high):
    shape = drawn.shape
    index_at = [jax.random.randint(jax.random.fold_in(stream_key, axis), (), 0, shape[axis]) for axis in range(len(shape))]
    drawn = drawn.at[tuple(index_at)].set(smallest)
    longest = shape.index(max(shape))
    index_at[longest] = (index_at[longest] + 1) % shape[longest]
    return drawn.at[tuple(index_at)].set(high)


def steps_of(rng, extent, cuts, low, high):
    def one(axis_at, parts):
        steps = jax.random.uniform(jax.random.fold_in(jax.random.fold_in(rng, 6), axis_at), (parts,), jnp.float32, low / len(cuts), high / len(cuts))
        return jnp.repeat(jnp.exp(steps), extent[axis_at] // parts).reshape((-1,) + (1,) * (len(extent) - axis_at - 1))

    level = one(*cuts[0])
    for cut in cuts[1:]:
        level = level * one(*cut)
    return level


def scatter_about(rng, dims, scale, limit, shards=(), kind=jnp.bfloat16):
    drawn = jax.random.normal(rng, dims, jnp.float32) * scale
    if len(shards) > 0:
        drawn = steps_of(rng, dims, shards, -0.22, 0.18) * drawn
    return jnp.clip(drawn, min=-limit, max=limit).astype(kind)


def setup_inputs(seed: int = 0) -> dict:
    arg_keys = jax.random.split(jax.random.key(seed), 7)
    return {
        "queries": draw_queries(jax.random.fold_in(arg_keys[6], 71), 0),
        "keys": draw_keys(jax.random.fold_in(arg_keys[6], 71), 0),
        "values": scatter_about(arg_keys[2], (TOKENS, HEADS * HD), 1.0, 6.0, ((0, 128),)),
        "grad_out": scatter_about(arg_keys[3], (TOKENS, HEADS * HD), 1.0, 6.0, ((0, 128),)),
        "pattern": place_ends((jax.random.randint(arg_keys[4], (NBLOCKS, LEVELS), 0, 4) < 3).astype(jnp.int32), jax.random.fold_in(arg_keys[4], 1), 0, 1),
        "phase": place_ends(jax.random.randint(arg_keys[5], (NBLOCKS, LEVELS), 0, 8), jax.random.fold_in(arg_keys[5], 1), 0, 7).astype(jnp.int32),
    }


NEG_FILL = -1.0e30


def block_terms(query_blk, key_set, value_set, grad_blk, allowed):
    scale_factor = HD ** -0.5
    logits = jnp.einsum("qhe,khe->hqk", query_blk.astype(jnp.float32), key_set.astype(jnp.float32)) * scale_factor
    logits = jnp.where(allowed[None], logits, NEG_FILL)
    row_max = jnp.max(logits, axis=2, keepdims=True)
    log_total = row_max + jnp.log(jnp.sum(jnp.exp(logits - row_max), axis=2, keepdims=True))
    probs = jnp.exp(logits - log_total)
    rounded = probs.astype(jnp.bfloat16).astype(jnp.float32)
    dprobs = jnp.einsum("qhe,khe->hqk", grad_blk.astype(jnp.float32), value_set.astype(jnp.float32))
    delta = jnp.sum(rounded * dprobs, axis=2, keepdims=True)
    dscores = (probs * (dprobs - delta)).astype(jnp.bfloat16).astype(jnp.float32)
    grad_q = jnp.einsum("hqk,khe->qhe", dscores, key_set.astype(jnp.float32)) * scale_factor
    grad_k = jnp.einsum("hqk,qhe->khe", dscores, query_blk.astype(jnp.float32)) * scale_factor
    grad_v = jnp.einsum("hqk,qhe->khe", rounded, grad_blk.astype(jnp.float32))
    return grad_q, grad_k, grad_v


def reference(queries, keys, values, grad_out, pattern, phase):
    block_total = TOKENS // BLK
    shape_four = (block_total, BLK, HEADS, HD)
    query_all = queries.reshape(shape_four)
    key_all = keys.reshape(shape_four)
    value_all = values.reshape(shape_four)
    grad_all = grad_out.reshape(shape_four)
    position = jnp.arange(BLK, dtype=jnp.int32)
    causal = position[:, None] >= position[None, :]

    def per_block(carried, block_id):
        dk_acc, dv_acc = carried
        key_parts = [key_all[block_id]]
        value_parts = [value_all[block_id]]
        allowed_parts = [causal]
        sources = []
        for level_num in range(LEVELS):
            distance = 2 ** level_num
            source = jnp.maximum(block_id - distance, 0).astype(jnp.int32)
            active = (block_id >= distance) & (pattern[block_id, level_num] == 1)
            keep = active & (position % distance == phase[block_id, level_num] % distance)
            key_parts.append(key_all[source])
            value_parts.append(value_all[source])
            allowed_parts.append(jnp.broadcast_to(keep[None, :], (BLK, BLK)))
            sources.append(source)
        grad_q, grad_k, grad_v = block_terms(query_all[block_id], jnp.concatenate(key_parts, axis=0),
                                             jnp.concatenate(value_parts, axis=0), grad_all[block_id],
                                             jnp.concatenate(allowed_parts, axis=1))
        dk_acc = dk_acc.at[block_id].add(grad_k[:BLK])
        dv_acc = dv_acc.at[block_id].add(grad_v[:BLK])
        for level_num in range(LEVELS):
            lower = (level_num + 1) * BLK
            piece_k = lax.optimization_barrier(grad_k[lower:lower + BLK].astype(jnp.bfloat16)).astype(jnp.float32)
            piece_v = lax.optimization_barrier(grad_v[lower:lower + BLK].astype(jnp.bfloat16)).astype(jnp.float32)
            dk_acc = dk_acc.at[sources[level_num]].add(piece_k)
            dv_acc = dv_acc.at[sources[level_num]].add(piece_v)
        return (dk_acc, dv_acc), grad_q.astype(jnp.bfloat16)

    zeros_acc = jnp.zeros(shape_four, jnp.float32)
    (dk_acc, dv_acc), dq_all = lax.scan(per_block, (zeros_acc, zeros_acc), jnp.arange(block_total, dtype=jnp.int32))
    flat = (TOKENS, HEADS * HD)
    return (dq_all.reshape(flat), dk_acc.astype(jnp.bfloat16).reshape(flat), dv_acc.astype(jnp.bfloat16).reshape(flat))
```

```python
import functools
import math

import jax
import jax.numpy as jnp
from jax import lax
from jax.experimental import pallas as pl
from jax.experimental.pallas import tpu as pltpu
from jax.sharding import Mesh, PartitionSpec as P

HD = 128
BLK = 384
HALF = 192
LEVELS = 4
LINE = 8
GROUP = 4
CHUNKS = 4
NEG = -1e30
SCALE = HD**-0.5
LOG2E = math.log2(math.e)
NEXT_L1 = BLK
NEXT_L2 = BLK + BLK // 2
NEXT_ROWS = NEXT_L2 + 3 * (BLK // 4)
FAR_ROWS = GROUP * (BLK // 8)
KEYS = BLK + BLK + BLK // 2 + BLK // 4 + BLK // 8
SEG = [0, BLK, 2 * BLK, 2 * BLK + BLK // 2, 2 * BLK + BLK // 2 + BLK // 4, KEYS]
OWN, NXT, AFT = 16, 32, 48
LINE_AXES = ("yh", "core", "yl")
GROUP_AXES = ("z", "x")
F32 = jnp.float32
BF16 = jnp.bfloat16


def dot(a, b, dims):
    return lax.dot_general(a, b, ((dims[0], dims[1]), ((), ())), preferred_element_type=F32)


def picker(stride, phase):
    rows = BLK // stride
    row = lax.broadcasted_iota(jnp.int32, (rows, BLK), 0)
    col = lax.broadcasted_iota(jnp.int32, (rows, BLK), 1)
    return jnp.where(col == row * stride + (phase & (stride - 1)), 1.0, 0.0).astype(BF16)


def spreader(stride, phase):
    cols = BLK // stride
    row = lax.broadcasted_iota(jnp.int32, (BLK, cols), 0)
    col = lax.broadcasted_iota(jnp.int32, (BLK, cols), 1)
    return jnp.where(row == col * stride + (phase & (stride - 1)), 1.0, 0.0).astype(BF16)


def pick(stride, phase, rows):
    return dot(picker(stride, phase), rows, ((1,), (0,))).astype(BF16)


def spread(stride, phase, rows):
    return dot(spreader(stride, phase), rows, ((1,), (0,)))


def kv_of(y_ref, block):
    at = pl.ds(2 * block, 2)
    return jnp.concatenate(
        [y_ref[at, 0, 0].reshape(BLK, HD), y_ref[at, 0, 1].reshape(BLK, HD)], axis=1
    )


def send_kernel(meta, y_ref, next_ref, far_ref):
    next_ref[0, 0:BLK] = kv_of(y_ref, 3)
    next_ref[0, NEXT_L1:NEXT_L2] = pick(2, meta[NXT + 1], kv_of(y_ref, 2))
    for b in range(3):
        lo = NEXT_L2 + b * 96
        next_ref[0, lo : lo + 96] = pick(4, meta[NXT + 4 * b + 2], kv_of(y_ref, b))
    for b in range(GROUP):
        far_ref[0, 48 * b : 48 * b + 48] = pick(8, meta[AFT + 4 * b + 3], kv_of(y_ref, b))


def main_kernel(meta, y_ref, next_ref, far_ref, dq_ref, acc_ref, rnext_ref, rfar_ref, kv, s, dp, p, ds, prev):
    b = pl.program_id(1)

    @pl.when(b == 0)
    def _():
        prev[...] = jnp.zeros_like(prev)
        p[0:BLK] = jnp.zeros((BLK, BLK), BF16)
        ds[0:BLK] = jnp.zeros((BLK, BLK), BF16)

    kv[0:BLK] = kv_of(y_ref, b)

    @pl.when(b == 0)
    def _():
        kv[SEG[1] : SEG[2]] = next_ref[0, 0:BLK]
        kv[SEG[2] : SEG[3]] = next_ref[0, NEXT_L1:NEXT_L2]

    @pl.when(b > 0)
    def _():
        kv[SEG[1] : SEG[2]] = kv_of(y_ref, b - 1)

    @pl.when(b == 1)
    def _():
        kv[SEG[2] : SEG[3]] = pick(2, meta[OWN + 4 * b + 1], next_ref[0, 0:BLK])

    @pl.when(b > 1)
    def _():
        kv[SEG[2] : SEG[3]] = pick(2, meta[OWN + 4 * b + 1], kv_of(y_ref, b - 2))

    l2_at = pl.ds(pl.multiple_of(NEXT_L2 + 96 * jnp.minimum(b, 2), 32), 96)
    l3_at = pl.ds(pl.multiple_of(48 * b, 16), 48)

    @pl.when(b < 3)
    def _():
        kv[SEG[3] : SEG[4]] = next_ref[0, l2_at]

    @pl.when(b == 3)
    def _():
        kv[SEG[3] : SEG[4]] = pick(4, meta[OWN + 4 * b + 2], next_ref[0, 0:BLK])

    kv[SEG[4] : SEG[5]] = far_ref[0, l3_at]

    at = pl.ds(2 * b, 2)
    q = y_ref[at, 0, 2].reshape(BLK, HD)
    do = y_ref[at, 0, 3].reshape(BLK, HD)
    s[...] = dot(kv[:, :HD], q, ((1,), (1,)))
    dp[...] = dot(kv[:, HD:], do, ((1,), (1,)))

    biases = [None] + [jnp.where(meta[4 * b + k] == 1, 0.0, NEG).astype(F32) for k in range(LEVELS)]
    row = lax.broadcasted_iota(jnp.int32, (128, 128), 0)
    col = lax.broadcasted_iota(jnp.int32, (128, 128), 1)
    upper = row <= col
    c = SCALE * LOG2E
    for i in range(3):
        lanes = slice(128 * i, 128 * i + 128)
        tiles = [(128 * j, 128 * j + 128, 0) for j in range(i + 1)]
        tiles += [(BLK + 128 * j, BLK + 128 * j + 128, 1) for j in range(3)]
        tiles += [(SEG[2], SEG[2] + 96, 2), (SEG[2] + 96, SEG[3], 2), (SEG[3], SEG[4], 3), (SEG[4], SEG[5], 4)]
        m = None
        for lo, hi, seg in tiles:
            t = s[lo:hi, lanes]
            if seg == 0 and lo == 128 * i:
                t = jnp.where(upper, t, NEG)
                s[lo:hi, lanes] = t
            t = jnp.max(t, axis=0, keepdims=True)
            if biases[seg] is not None:
                t = t + biases[seg]
            m = t if m is None else jnp.maximum(m, t)
        m = m * c
        total = jnp.zeros((1, 128), F32)
        delta = jnp.zeros((1, 128), F32)
        for lo, hi, seg in tiles:
            shift = m if biases[seg] is None else m - biases[seg]
            e = jnp.exp2(s[lo:hi, lanes] * c - shift)
            s[lo:hi, lanes] = e
            total = total + jnp.sum(e, axis=0, keepdims=True)
            delta = delta + jnp.sum(e * dp[lo:hi, lanes], axis=0, keepdims=True)
        inv = 1.0 / total
        delta = delta * inv
        for lo, hi, seg in tiles:
            prob = s[lo:hi, lanes] * inv
            p[lo:hi, lanes] = prob.astype(BF16)
            ds[lo:hi, lanes] = (prob * (dp[lo:hi, lanes] - delta)).astype(BF16)

    dq_ref[0, 0] = (dot(ds[...], kv[:, :HD], ((0,), (0,))) * SCALE).astype(BF16)

    def grads(k):
        rows = slice(SEG[k], SEG[k + 1])
        dk = dot(ds[rows], q, ((1,), (0,))) * SCALE
        dv = dot(p[rows], do, ((1,), (0,)))
        return jnp.concatenate([dk, dv], axis=1)

    acc_ref[0, b] = grads(0)
    near = grads(1)

    @pl.when(b == 0)
    def _():
        prev[...] += near

    @pl.when(b > 0)
    def _():
        acc_ref[0, b - 1] += near

    term = grads(2).astype(BF16)

    @pl.when(b == 0)
    def _():
        rnext_ref[0, NEXT_L1:NEXT_L2] = term

    @pl.when(b == 1)
    def _():
        prev[...] += spread(2, meta[OWN + 4 * b + 1], term)

    @pl.when(b > 1)
    def _():
        acc_ref[0, b - 2] += spread(2, meta[OWN + 4 * b + 1], term)

    term2 = grads(3).astype(BF16)

    @pl.when(b < 3)
    def _():
        rnext_ref[0, l2_at] = term2

    @pl.when(b == 3)
    def _():
        rnext_ref[0, 0:BLK] = (prev[...] + spread(4, meta[OWN + 4 * b + 2], term2)).astype(BF16)

    rfar_ref[0, l3_at] = grads(4).astype(BF16)


def join_kernel(meta, acc_ref, dq_ref, rnext_ref, rfar_ref, z_ref, t):
    b = pl.program_id(1)
    l2_at = pl.ds(pl.multiple_of(NEXT_L2 + 96 * jnp.minimum(b, 2), 32), 96)
    l3_at = pl.ds(pl.multiple_of(48 * b, 16), 48)
    t[...] = acc_ref[0, 0] + spread(8, meta[AFT + 4 * b + 3], rfar_ref[0, l3_at])

    @pl.when(b < 3)
    def _():
        t[...] += spread(4, meta[NXT + 4 * b + 2], rnext_ref[0, l2_at])

    @pl.when(b == 2)
    def _():
        t[...] += spread(2, meta[NXT + 1], rnext_ref[0, NEXT_L1:NEXT_L2])

    @pl.when(b == 3)
    def _():
        t[...] += rnext_ref[0, 0:BLK].astype(F32)

    z_ref[:, 0, 0] = dq_ref[0, 0].reshape(2, HALF, HD)
    z_ref[:, 0, 1] = t[:, :HD].astype(BF16).reshape(2, HALF, HD)
    z_ref[:, 0, 2] = t[:, HD:].astype(BF16).reshape(2, HALF, HD)


SMEM = pl.BlockSpec(memory_space=pltpu.SMEM)


def params(mib):
    return pltpu.CompilerParams(
        dimension_semantics=("arbitrary", "arbitrary"), vmem_limit_bytes=mib * 2**20
    )


def whole(shape):
    return pl.BlockSpec((1, *shape), lambda h, b: (h,) + (0,) * len(shape))


def y_spec(arrays):
    return pl.BlockSpec((LINE, 1, arrays, HALF, HD), lambda h, b: (0, h, 0, 0, 0))


def rows_to_send(meta, y):
    heads = y.shape[1]
    return pl.pallas_call(
        send_kernel,
        grid=(heads, 1),
        in_specs=[SMEM, y_spec(2)],
        out_specs=[whole((NEXT_ROWS, 2 * HD)), whole((FAR_ROWS, 2 * HD))],
        out_shape=[
            jax.ShapeDtypeStruct((heads, NEXT_ROWS, 2 * HD), BF16),
            jax.ShapeDtypeStruct((heads, FAR_ROWS, 2 * HD), BF16),
        ],
        compiler_params=params(16),
        cost_estimate=pl.CostEstimate(flops=heads * 2**27, bytes_accessed=heads * 2**21, transcendentals=0),
        name="rows_to_send",
    )(meta, y)


def attention(meta, y, near, far):
    heads = y.shape[1]
    return pl.pallas_call(
        main_kernel,
        grid=(heads, GROUP),
        in_specs=[SMEM, y_spec(4), whole((NEXT_ROWS, 2 * HD)), whole((FAR_ROWS, 2 * HD))],
        out_specs=[
            pl.BlockSpec((1, 1, BLK, HD), lambda h, b: (h, b, 0, 0)),
            whole((GROUP, BLK, 2 * HD)),
            whole((NEXT_ROWS, 2 * HD)),
            whole((FAR_ROWS, 2 * HD)),
        ],
        out_shape=[
            jax.ShapeDtypeStruct((heads, GROUP, BLK, HD), BF16),
            jax.ShapeDtypeStruct((heads, GROUP, BLK, 2 * HD), F32),
            jax.ShapeDtypeStruct((heads, NEXT_ROWS, 2 * HD), BF16),
            jax.ShapeDtypeStruct((heads, FAR_ROWS, 2 * HD), BF16),
        ],
        scratch_shapes=[
            pltpu.VMEM((KEYS, 2 * HD), BF16),
            pltpu.VMEM((KEYS, BLK), F32),
            pltpu.VMEM((KEYS, BLK), F32),
            pltpu.VMEM((KEYS, BLK), BF16),
            pltpu.VMEM((KEYS, BLK), BF16),
            pltpu.VMEM((BLK, 2 * HD), F32),
        ],
        compiler_params=params(32),
        cost_estimate=pl.CostEstimate(
            flops=heads * GROUP * BLK * KEYS * HD * 10 * 4,
            bytes_accessed=heads * 5 * 2**20,
            transcendentals=heads * GROUP * BLK * KEYS,
        ),
        name="attention",
    )(meta, y, near, far)


def joined(meta, acc, dq, near, far):
    heads = acc.shape[0]
    return pl.pallas_call(
        join_kernel,
        grid=(heads, GROUP),
        in_specs=[
            SMEM,
            pl.BlockSpec((1, 1, BLK, 2 * HD), lambda h, b: (h, b, 0, 0)),
            pl.BlockSpec((1, 1, BLK, HD), lambda h, b: (h, b, 0, 0)),
            whole((NEXT_ROWS, 2 * HD)),
            whole((FAR_ROWS, 2 * HD)),
        ],
        out_specs=pl.BlockSpec((2, 1, 3, HALF, HD), lambda h, b: (b, h, 0, 0, 0)),
        out_shape=jax.ShapeDtypeStruct((LINE, heads, 3, HALF, HD), BF16),
        scratch_shapes=[pltpu.VMEM((BLK, 2 * HD), F32)],
        compiler_params=params(16),
        cost_estimate=pl.CostEstimate(flops=heads * 2**28, bytes_accessed=heads * 2**22, transcendentals=0),
        name="joined",
    )(meta, acc, dq, near, far)


def shift(value, steps):
    count = lax.axis_size(GROUP_AXES)
    pairs = [(i, i + steps) for i in range(count) if 0 <= i + steps < count]
    return lax.ppermute(value, GROUP_AXES, pairs)


def both(value, axis):
    other = lax.ppermute(value, axis, [(0, 1), (1, 0)])
    first = lax.axis_index(axis) == 0
    return jnp.stack([jnp.where(first, value, other), jnp.where(first, other, value)])


def meta_of(pattern, phase):
    own = jnp.concatenate([pattern, phase], axis=1)
    rows = jnp.concatenate([own, shift(own, -1), shift(own, -2)], axis=0)
    rows = both(both(rows, "core"), "yh").reshape(GROUP, 3, 2 * LEVELS)
    block = lax.axis_index(GROUP_AXES) * GROUP + jnp.arange(GROUP)
    distance = 2 ** jnp.arange(LEVELS)
    active = (rows[:, 0, :LEVELS] == 1) & (block[:, None] >= distance[None, :])
    phases = rows[:, :, LEVELS:].transpose(1, 0, 2)
    return jnp.concatenate([active.astype(jnp.int32).reshape(-1), phases.reshape(-1)])


def body(queries, keys, values, grad_out, pattern, phase):
    meta = meta_of(pattern, phase)
    width = queries.shape[1] // CHUNKS
    heads = width // (LINE * HD)
    results = []
    for chunk in range(CHUNKS):
        cols = slice(chunk * width, (chunk + 1) * width)
        x = jnp.stack([a[:, cols] for a in (keys, values, queries, grad_out)])
        x = x.reshape(4, HALF, LINE, heads, HD).transpose(2, 3, 0, 1, 4)
        y = lax.all_to_all(x, LINE_AXES, 0, 0, tiled=True)
        near, far = rows_to_send(meta, y)
        near, far = shift(near, 1), shift(far, 2)
        dq, acc, near, far = attention(meta, y, near, far)
        near, far = shift(near, -1), shift(far, -2)
        z = joined(meta, acc, dq, near, far)
        w = lax.all_to_all(z, LINE_AXES, 0, 0, tiled=True)
        results.append(w.transpose(2, 3, 0, 1, 4).reshape(3, HALF, width))
    return tuple(jnp.concatenate([r[i] for r in results], axis=1) for i in range(3))


def solution(mesh):
    sizes = (4, 4, 2, 2, 2)
    line = Mesh(mesh.devices.reshape(sizes), ("z", "x", "yh", "core", "yl"))
    ctx = ("z", "x", "yh", "core")
    tokens = P((*ctx, "yl"), None)
    return jax.shard_map(
        body,
        mesh=line,
        in_specs=(tokens,) * 4 + (P(ctx, None),) * 2,
        out_specs=(tokens,) * 3,
        check_vma=False,
    )
```

```python
import functools
import math

import jax
import jax.numpy as jnp
from jax import lax
from jax.experimental import pallas as pl
from jax.experimental.pallas import tpu as pltpu
from jax.sharding import Mesh, PartitionSpec as P

HD = 128
BLK = 384
HALF = 192
LEVELS = 4
LINE = 8
GROUP = 4
HEADS = 4
PAIR = 2
NEG = -1e30
SCALE = HD**-0.5
LOG2E = math.log2(math.e)
NEXT_L1 = BLK
NEXT_L2 = BLK + BLK // 2
NEXT_ROWS = NEXT_L2 + 3 * (BLK // 4)
FAR_ROWS = GROUP * (BLK // 8)
KEYS = BLK + BLK + BLK // 2 + BLK // 4 + BLK // 8
SEG = [0, BLK, 2 * BLK, 2 * BLK + BLK // 2, 2 * BLK + BLK // 2 + BLK // 4, KEYS]
OWN, NXT, AFT = 16, 32, 48
LINE_AXES = ("yh", "core", "yl")
GROUP_AXES = ("z", "x")
F32 = jnp.float32
BF16 = jnp.bfloat16


def dot(a, b, dims):
    return lax.dot_general(a, b, ((dims[0], dims[1]), ((), ())), preferred_element_type=F32)


def picker(stride, phase):
    rows = BLK // stride
    row = lax.broadcasted_iota(jnp.int32, (rows, BLK), 0)
    col = lax.broadcasted_iota(jnp.int32, (rows, BLK), 1)
    return jnp.where(col == row * stride + (phase & (stride - 1)), 1.0, 0.0).astype(BF16)


def spreader(stride, phase):
    cols = BLK // stride
    row = lax.broadcasted_iota(jnp.int32, (BLK, cols), 0)
    col = lax.broadcasted_iota(jnp.int32, (BLK, cols), 1)
    return jnp.where(row == col * stride + (phase & (stride - 1)), 1.0, 0.0).astype(BF16)


def pick(stride, phase, rows):
    return dot(picker(stride, phase), rows, ((1,), (0,))).astype(BF16)


def spread(stride, phase, rows):
    return dot(spreader(stride, phase), rows, ((1,), (0,)))


def kv_of(y_ref, block):
    at = slice(2 * block, 2 * block + 2)
    return jnp.concatenate([y_ref[at, 0].reshape(BLK, HD), y_ref[at, 1].reshape(BLK, HD)], axis=1)


def send_kernel(pair, meta, y_ref, *refs):
    outs = refs[-PAIR - (pair == 0) :]
    for i in range(PAIR):
        h = pair * PAIR + i
        y, near_ref = y_ref.at[:, :, :, h * HD : (h + 1) * HD], outs[i]
        near_ref[0, 0:BLK] = kv_of(y, 3)
        near_ref[0, NEXT_L1:NEXT_L2] = pick(2, meta[NXT + 1], kv_of(y, 2))
        for b in range(3):
            lo = NEXT_L2 + b * 96
            near_ref[0, lo : lo + 96] = pick(4, meta[NXT + 4 * b + 2], kv_of(y, b))
    if pair == 0:
        for h in range(HEADS):
            y = y_ref.at[:, :, :, h * HD : (h + 1) * HD]
            for b in range(GROUP):
                outs[PAIR][h, 48 * b : 48 * b + 48] = pick(8, meta[AFT + 4 * b + 3], kv_of(y, b))


def emit(pieces):
    for piece in pieces:
        piece()


def main_kernel(meta, y_ref, w_ref, next_ref, far_ref, *refs):
    dq_ref, acc_ref, rnext_ref, rfar_ref, kvs, ss, dps, ps, dss, prev = refs[-10:]
    row_tiles = [(lo, min(lo + 128, KEYS)) for lo in range(0, KEYS, 128)]

    def q_of(b):
        return w_ref[2 * b : 2 * b + 2, 0].reshape(BLK, HD)

    def g_of(b):
        return w_ref[2 * b : 2 * b + 2, 1].reshape(BLK, HD)

    def gather(b):
        kv = kvs.at[b % 2]
        last = [None, lambda: next_ref[0, 0:BLK]] + [functools.partial(kv_of, y_ref, i) for i in range(b + 1)]
        own, one, two = last[b + 2], last[b + 1], last[b]
        kv[0:BLK] = own()
        kv[SEG[1] : SEG[2]] = one()
        if two is None:
            kv[SEG[2] : SEG[3]] = next_ref[0, NEXT_L1:NEXT_L2]
        else:
            kv[SEG[2] : SEG[3]] = pick(2, meta[OWN + 4 * b + 1], two())
        if b < 3:
            kv[SEG[3] : SEG[4]] = next_ref[0, NEXT_L2 + 96 * b : NEXT_L2 + 96 * b + 96]
        else:
            kv[SEG[3] : SEG[4]] = pick(4, meta[OWN + 4 * b + 2], next_ref[0, 0:BLK])
        kv[SEG[4] : SEG[5]] = far_ref[0, 48 * b : 48 * b + 48]

    def products(b):
        kv, s, dp = kvs.at[b % 2], ss.at[b % 2], dps.at[b % 2]
        yield lambda: gather(b)

        def tile(lo, hi, which):
            if which:
                dp[lo:hi] = dot(kv[lo:hi, HD:], g_of(b), ((1,), (1,)))
            else:
                s[lo:hi] = dot(kv[lo:hi, :HD], q_of(b), ((1,), (1,)))

        for which in (0, 1):
            for lo, hi in row_tiles:
                yield functools.partial(tile, lo, hi, which)

    def softmax(b):
        s, dp, p, ds = ss.at[b % 2], dps.at[b % 2], ps.at[b % 2], dss.at[b % 2]
        biases = [None] + [jnp.where(meta[4 * b + k] == 1, 0.0, NEG).astype(F32) for k in range(LEVELS)]
        row = lax.broadcasted_iota(jnp.int32, (128, 128), 0)
        col = lax.broadcasted_iota(jnp.int32, (128, 128), 1)
        upper = row <= col
        c = SCALE * LOG2E
        for i in range(3):
            lanes = slice(128 * i, 128 * i + 128)
            tiles = [(128 * j, 128 * j + 128, 0) for j in range(i + 1)]
            tiles += [(BLK + 128 * j, BLK + 128 * j + 128, 1) for j in range(3)]
            tiles += [(SEG[2], SEG[2] + 96, 2), (SEG[2] + 96, SEG[3], 2), (SEG[3], SEG[4], 3), (SEG[4], SEG[5], 4)]
            st = dict(m=None, total=None, delta=None)

            def top(lo, hi, seg, i=i, lanes=lanes, st=st):
                t = s[lo:hi, lanes]
                if seg == 0 and lo == 128 * i:
                    t = jnp.where(upper, t, NEG)
                t = jnp.max(t, axis=0, keepdims=True)
                if biases[seg] is not None:
                    t = t + biases[seg]
                st["m"] = t if st["m"] is None else jnp.maximum(st["m"], t)

            def exps(lo, hi, seg, i=i, lanes=lanes, st=st):
                m = st["m"] * c
                shift = m if biases[seg] is None else m - biases[seg]
                t = s[lo:hi, lanes] * c - shift
                if seg == 0 and lo == 128 * i:
                    t = jnp.where(upper, t, NEG)
                e = jnp.exp2(t)
                s[lo:hi, lanes] = e
                total = jnp.sum(e, axis=0, keepdims=True)
                delta = jnp.sum(e * dp[lo:hi, lanes], axis=0, keepdims=True)
                st["total"] = total if st["total"] is None else st["total"] + total
                st["delta"] = delta if st["delta"] is None else st["delta"] + delta

            def norm(st=st):
                st["inv"] = 1.0 / st["total"]
                st["delta"] = st["delta"] * st["inv"]

            def scores(lo, hi, lanes=lanes, st=st):
                prob = s[lo:hi, lanes] * st["inv"]
                p[lo:hi, lanes] = prob.astype(BF16)
                ds[lo:hi, lanes] = (prob * (dp[lo:hi, lanes] - st["delta"])).astype(BF16)

            for lo, hi, seg in tiles:
                yield functools.partial(top, lo, hi, seg)
            for lo, hi, seg in tiles:
                yield functools.partial(exps, lo, hi, seg)
            yield norm
            for lo, hi, seg in tiles:
                yield functools.partial(scores, lo, hi)

    def gradients(b):
        kv, p, ds = kvs.at[b % 2], ps.at[b % 2], dss.at[b % 2]

        def queries(i):
            lanes = slice(128 * i, 128 * i + 128)
            part = dot(ds[:, lanes], kv[:, :HD], ((0,), (0,))) * SCALE
            dq_ref[0, b, lanes] = part.astype(BF16)

        def pair(lo, hi):
            dk = dot(ds[lo:hi], q_of(b), ((1,), (0,))) * SCALE
            dv = dot(p[lo:hi], g_of(b), ((1,), (0,)))
            return jnp.concatenate([dk, dv], axis=1)

        def own(j):
            acc_ref[0, b, 128 * j : 128 * j + 128] = pair(128 * j, 128 * j + 128)

        def near(j):
            rows = slice(128 * j, 128 * j + 128)
            term = pair(BLK + 128 * j, BLK + 128 * j + 128)
            if b == 0:
                prev[rows] = term
            else:
                acc_ref[0, b - 1, rows] += term

        def two():
            term = pair(SEG[2], SEG[3]).astype(BF16)
            if b == 0:
                rnext_ref[0, NEXT_L1:NEXT_L2] = term
            elif b == 1:
                prev[...] += spread(2, meta[OWN + 4 * b + 1], term)
            else:
                acc_ref[0, b - 2] += spread(2, meta[OWN + 4 * b + 1], term)

        def four():
            term = pair(SEG[3], SEG[4]).astype(BF16)
            if b < 3:
                rnext_ref[0, NEXT_L2 + 96 * b : NEXT_L2 + 96 * b + 96] = term
            else:
                rnext_ref[0, 0:BLK] = (prev[...] + spread(4, meta[OWN + 4 * b + 2], term)).astype(BF16)

        def eight():
            rfar_ref[0, 48 * b : 48 * b + 48] = pair(SEG[4], SEG[5]).astype(BF16)

        for j in range(3):
            yield functools.partial(own, j)
            yield functools.partial(near, j)
        yield two
        yield four
        yield eight
        for i in range(3):
            yield functools.partial(queries, i)

    for i in range(2):
        ps[i, 0:BLK] = jnp.zeros((BLK, BLK), BF16)
        dss[i, 0:BLK] = jnp.zeros((BLK, BLK), BF16)
    emit(products(0))
    for b in range(GROUP):
        emit(softmax(b))
        if b + 1 < GROUP:
            emit(products(b + 1))
        emit(gradients(b))


def join_kernel(meta, acc_ref, dq_ref, near_ref, far_ref, *refs):
    z_ref, t = refs[-2:]
    b = pl.program_id(0)
    l2_at = pl.ds(pl.multiple_of(NEXT_L2 + 96 * jnp.minimum(b, 2), 32), 96)
    l3_at = pl.ds(pl.multiple_of(48 * b, 16), 48)
    t[...] = acc_ref[0, 0] + spread(8, meta[AFT + 4 * b + 3], far_ref[0, l3_at])

    @pl.when(b < 3)
    def _():
        t[...] += spread(4, meta[NXT + 4 * b + 2], near_ref[0, l2_at])

    @pl.when(b == 2)
    def _():
        t[...] += spread(2, meta[NXT + 1], near_ref[0, NEXT_L1:NEXT_L2])

    @pl.when(b == 3)
    def _():
        t[...] += near_ref[0, 0:BLK].astype(F32)

    z_ref[:, 0] = dq_ref[0, 0].reshape(2, HALF, HD)
    z_ref[:, 1] = t[:, :HD].astype(BF16).reshape(2, HALF, HD)
    z_ref[:, 2] = t[:, HD:].astype(BF16).reshape(2, HALF, HD)


def columns(device, first, count):
    return pl.ds((device * HEADS + first) * HD, count * HD)


def pack_kernel(parts, *refs):
    arrays, outs, (held, ins, sems) = refs[:2], refs[2:-3], refs[-3:]
    reads = [pltpu.make_async_copy(a, held.at[i], ins.at[i]) for i, a in enumerate(arrays)]
    for read in reads:
        read.start()
    writes = []
    for i, read in enumerate(reads):
        read.wait()
        for j, part in enumerate(parts):
            for g in range(LINE):
                write = pltpu.make_async_copy(
                    held.at[i, :, columns(g, *part)], outs[j].at[g, i], sems.at[i, j, g]
                )
                write.start()
                writes.append(write)
    for write in writes:
        write.wait()


def unpack_kernel(head, w_ref, *refs):
    outs, (held, ins, sems) = refs[-6:-3], refs[-3:]
    reads = [pltpu.make_async_copy(w_ref.at[g], held.at[g], ins.at[g]) for g in range(LINE)]
    for read in reads:
        read.start()
    writes = []
    for g, read in enumerate(reads):
        read.wait()
        for i in range(3):
            write = pltpu.make_async_copy(held.at[g, i], outs[i].at[:, columns(g, head, 1)], sems.at[g, i])
            write.start()
            writes.append(write)
    for write in writes:
        write.wait()


SMEM = pl.BlockSpec(memory_space=pltpu.SMEM)
ANY = pl.BlockSpec(memory_space=pl.ANY)


def params(mib, axes=1):
    return pltpu.CompilerParams(
        dimension_semantics=("arbitrary",) * axes, vmem_limit_bytes=mib * 2**20
    )


def whole(shape):
    return pl.BlockSpec(shape, lambda b: (0,) * len(shape))


def y_spec(head, arrays):
    return pl.BlockSpec((LINE, 1, arrays, HALF, HD), lambda b: (0, head, 0, 0, 0))


def cost(flops, size, exps=0):
    return pl.CostEstimate(flops=int(flops), bytes_accessed=int(size), transcendentals=int(exps))


NEXT = jax.ShapeDtypeStruct((1, NEXT_ROWS, 2 * HD), BF16)
FAR = jax.ShapeDtypeStruct((1, FAR_ROWS, 2 * HD), BF16)


def packed(arrays, parts):
    widths = [count * HD for _, count in parts]
    return pl.pallas_call(
        functools.partial(pack_kernel, parts),
        in_specs=[ANY] * 2,
        out_specs=[ANY] * len(parts),
        out_shape=[jax.ShapeDtypeStruct((LINE, 2, HALF, width), BF16) for width in widths],
        scratch_shapes=[
            pltpu.VMEM((2, HALF, LINE * HEADS * HD), BF16),
            pltpu.SemaphoreType.DMA((2,)),
            pltpu.SemaphoreType.DMA((2, len(parts), LINE)),
        ],
        compiler_params=pltpu.CompilerParams(vmem_limit_bytes=60 * 2**20),
        cost_estimate=cost(0, 2**23),
        name="packed",
    )(*arrays)


def unpacked(w, head, into):
    into = tuple(into)
    return pl.pallas_call(
        functools.partial(unpack_kernel, head),
        in_specs=[ANY] * (1 + len(into)),
        out_specs=[ANY] * 3,
        out_shape=[jax.ShapeDtypeStruct((HALF, LINE * HEADS * HD), BF16)] * 3,
        input_output_aliases={1 + i: i for i in range(len(into))},
        scratch_shapes=[
            pltpu.VMEM((LINE, 3, HALF, HD), BF16),
            pltpu.SemaphoreType.DMA((LINE,)),
            pltpu.SemaphoreType.DMA((LINE, 3)),
        ],
        compiler_params=pltpu.CompilerParams(vmem_limit_bytes=60 * 2**20),
        cost_estimate=cost(0, 2**23),
        name="unpacked",
    )(w, *into)


def rows_to_send(meta, y, pair, after=()):
    far = (HEADS, FAR_ROWS, 2 * HD)
    first = pair == 0
    return pl.pallas_call(
        functools.partial(send_kernel, pair),
        grid=(1,),
        in_specs=[SMEM, whole(y.shape)] + [ANY] * len(after),
        out_specs=[whole(NEXT.shape)] * PAIR + [whole(far)] * first,
        out_shape=[NEXT] * PAIR + [jax.ShapeDtypeStruct(far, BF16)] * first,
        compiler_params=params(32),
        cost_estimate=cost(2**29, 2**23),
        name="rows_to_send",
    )(meta, y, *after)


def attention(meta, y, w, head, near, far, after=()):
    at = head % PAIR
    return pl.pallas_call(
        main_kernel,
        grid=(1,),
        in_specs=[
            SMEM,
            pl.BlockSpec((LINE, 2, HALF, HD), lambda b: (0, 0, 0, head)),
            pl.BlockSpec((LINE, 2, HALF, HD), lambda b: (0, 0, 0, at)),
            whole(NEXT.shape),
            pl.BlockSpec((1, FAR_ROWS, 2 * HD), lambda b: (head, 0, 0)),
        ]
        + [ANY] * len(after),
        out_specs=[
            whole((1, GROUP, BLK, HD)),
            whole((1, GROUP, BLK, 2 * HD)),
            whole(NEXT.shape),
            whole(FAR.shape),
        ],
        out_shape=[
            jax.ShapeDtypeStruct((1, GROUP, BLK, HD), BF16),
            jax.ShapeDtypeStruct((1, GROUP, BLK, 2 * HD), F32),
            NEXT,
            FAR,
        ],
        scratch_shapes=[
            pltpu.VMEM((2, KEYS, 2 * HD), BF16),
            pltpu.VMEM((2, KEYS, BLK), F32),
            pltpu.VMEM((2, KEYS, BLK), F32),
            pltpu.VMEM((2, KEYS, BLK), BF16),
            pltpu.VMEM((2, KEYS, BLK), BF16),
            pltpu.VMEM((BLK, 2 * HD), F32),
        ],
        compiler_params=params(32),
        cost_estimate=cost(GROUP * BLK * KEYS * HD * 30, 5 * 2**20, GROUP * BLK * KEYS),
        name="attention",
    )(meta, y, w, near, far, *after)


def joined(meta, acc, dq, near, far, after=()):
    return pl.pallas_call(
        join_kernel,
        grid=(GROUP,),
        in_specs=[
            SMEM,
            pl.BlockSpec((1, 1, BLK, 2 * HD), lambda b: (0, b, 0, 0)),
            pl.BlockSpec((1, 1, BLK, HD), lambda b: (0, b, 0, 0)),
            whole(NEXT.shape),
            whole(FAR.shape),
        ]
        + [ANY] * len(after),
        out_specs=pl.BlockSpec((2, 3, HALF, HD), lambda b: (b, 0, 0, 0)),
        out_shape=jax.ShapeDtypeStruct((LINE, 3, HALF, HD), BF16),
        scratch_shapes=[pltpu.VMEM((BLK, 2 * HD), F32)],
        compiler_params=params(16),
        cost_estimate=cost(2**29, 2**23),
        name="joined",
    )(meta, acc, dq, near, far, *after)


def shift(value, steps):
    count = lax.axis_size(GROUP_AXES)
    pairs = [(i, i + steps) for i in range(count) if 0 <= i + steps < count]
    return lax.ppermute(value, GROUP_AXES, pairs)


def both(value, axis):
    other = lax.ppermute(value, axis, [(0, 1), (1, 0)])
    first = lax.axis_index(axis) == 0
    return jnp.stack([jnp.where(first, value, other), jnp.where(first, other, value)])


def meta_of(pattern, phase):
    own = jnp.concatenate([pattern, phase], axis=1)
    rows = jnp.concatenate([own, shift(own, -1), shift(own, -2)], axis=0)
    rows = both(both(rows, "core"), "yh").reshape(GROUP, 3, 2 * LEVELS)
    block = lax.axis_index(GROUP_AXES) * GROUP + jnp.arange(GROUP)
    distance = 2 ** jnp.arange(LEVELS)
    active = (rows[:, 0, :LEVELS] == 1) & (block[:, None] >= distance[None, :])
    phases = rows[:, :, LEVELS:].transpose(1, 0, 2)
    return jnp.concatenate([active.astype(jnp.int32).reshape(-1), phases.reshape(-1)])


def exchange(x):
    return lax.all_to_all(x, LINE_AXES, 0, 0, tiled=True)


def body(queries, keys, values, grad_out, pattern, phase):
    (x,) = packed((keys, values), ((0, HEADS),))
    y = exchange(x)
    meta = meta_of(pattern, phase)
    w = [exchange(x) for x in packed((queries, grad_out), ((0, PAIR), (PAIR, PAIR)))]
    near0, near1, far = rows_to_send(meta, y, 0)
    far, near0, near1 = shift(far, 2), shift(near0, 1), shift(near1, 1)

    def grads(head, near, after=()):
        dq, acc, back, far_back = attention(meta, y, w[head // PAIR], head, near, far, after)
        return acc, dq, shift(back, -1), shift(far_back, -2)

    g0 = grads(0, near0)
    near2, near3 = rows_to_send(meta, y, 1, (g0[0],))
    near2, near3 = shift(near2, 1), shift(near3, 1)
    g1 = grads(1, near1, (g0[0],))
    z0 = joined(meta, *g0, (g1[0],))
    o0 = exchange(z0)
    g2 = grads(2, near2, (z0,))
    z1 = joined(meta, *g1, (g2[0],))
    o1 = exchange(z1)
    g3 = grads(3, near3, (z1, o0))
    z2 = joined(meta, *g2, (g3[0],))
    o2 = exchange(z2)
    z3 = joined(meta, *g3, (z2, o1))
    out = ()
    for head, o in enumerate((o0, o1, o2, exchange(z3))):
        out = unpacked(o, head, out)
    return tuple(out)


def solution(mesh):
    sizes = (4, 4, 2, 2, 2)
    line = Mesh(mesh.devices.reshape(sizes), ("z", "x", "yh", "core", "yl"))
    ctx = ("z", "x", "yh", "core")
    tokens = P((*ctx, "yl"), None)
    return jax.shard_map(
        body,
        mesh=line,
        in_specs=(tokens,) * 4 + (P(ctx, None),) * 2,
        out_specs=(tokens,) * 3,
        check_vma=False,
    )
```

```python
import functools
import math

import jax
import jax.numpy as jnp
from jax import lax
from jax.experimental import pallas as pl
from jax.experimental.pallas import tpu as pltpu
from jax.sharding import Mesh, PartitionSpec as P

HD = 128
BLK = 384
HALF = 192
LEVELS = 4
LINE = 8
GROUP = 4
PAIR = 2
NEG = -1e30
COST = 30
SCALE = HD**-0.5
LOG2E = math.log2(math.e)
NEXT_L1 = BLK
NEXT_L2 = BLK + BLK // 2
NEXT_ROWS = NEXT_L2 + 3 * (BLK // 4)
FAR_ROWS = GROUP * (BLK // 8)
KEYS = BLK + BLK + BLK // 2 + BLK // 4 + BLK // 8
SEG = [0, BLK, 2 * BLK, 2 * BLK + BLK // 2, 2 * BLK + BLK // 2 + BLK // 4, KEYS]
OWN, NXT, AFT = 16, 32, 48
LINE_AXES = ("yh", "core", "yl")
GROUP_AXES = ("z", "x")
F32 = jnp.float32
BF16 = jnp.bfloat16


def dot(a, b, dims):
    return lax.dot_general(a, b, ((dims[0], dims[1]), ((), ())), preferred_element_type=F32)


def picker(stride, phase):
    rows = BLK // stride
    row = lax.broadcasted_iota(jnp.int32, (rows, BLK), 0)
    col = lax.broadcasted_iota(jnp.int32, (rows, BLK), 1)
    return jnp.where(col == row * stride + (phase & (stride - 1)), 1.0, 0.0).astype(BF16)


def spreader(stride, phase):
    cols = BLK // stride
    row = lax.broadcasted_iota(jnp.int32, (BLK, cols), 0)
    col = lax.broadcasted_iota(jnp.int32, (BLK, cols), 1)
    return jnp.where(row == col * stride + (phase & (stride - 1)), 1.0, 0.0).astype(BF16)


def pick(stride, phase, rows):
    return dot(picker(stride, phase), rows, ((1,), (0,))).astype(BF16)


def spread(stride, phase, rows):
    return dot(spreader(stride, phase), rows, ((1,), (0,)))


def kv_of(y_ref, block):
    at = slice(2 * block, 2 * block + 2)
    return jnp.concatenate([y_ref[at, 0].reshape(BLK, HD), y_ref[at, 1].reshape(BLK, HD)], axis=1)


def send_kernel(meta, y_ref, near_ref, far_ref):
    for h in range(PAIR):
        y = y_ref.at[:, :, :, h * HD : (h + 1) * HD]
        near_ref[h, 0:BLK] = kv_of(y, 3)
        near_ref[h, NEXT_L1:NEXT_L2] = pick(2, meta[NXT + 1], kv_of(y, 2))
        for b in range(3):
            lo = NEXT_L2 + b * 96
            near_ref[h, lo : lo + 96] = pick(4, meta[NXT + 4 * b + 2], kv_of(y, b))
        for b in range(GROUP):
            far_ref[h, 48 * b : 48 * b + 48] = pick(8, meta[AFT + 4 * b + 3], kv_of(y, b))


def emit(pieces):
    for piece in pieces:
        piece()


def main_kernel(meta, y_ref, w_ref, next_ref, far_ref, *refs):
    dq_ref, acc_ref, rnext_ref, rfar_ref, kvs, ss, dps, ps, dss, prev = refs[-10:]

    def q_of(b):
        return w_ref[2 * b : 2 * b + 2, 0].reshape(BLK, HD)

    def g_of(b):
        return w_ref[2 * b : 2 * b + 2, 1].reshape(BLK, HD)

    def gather(b):
        kv = kvs.at[b % 2]
        last = [None, lambda: next_ref[0, 0:BLK]] + [functools.partial(kv_of, y_ref, i) for i in range(b + 1)]
        own, one, two = last[b + 2], last[b + 1], last[b]
        kv[0:BLK] = own()
        kv[SEG[1] : SEG[2]] = one()
        if two is None:
            kv[SEG[2] : SEG[3]] = next_ref[0, NEXT_L1:NEXT_L2]
        else:
            kv[SEG[2] : SEG[3]] = pick(2, meta[OWN + 4 * b + 1], two())
        if b < 3:
            kv[SEG[3] : SEG[4]] = next_ref[0, NEXT_L2 + 96 * b : NEXT_L2 + 96 * b + 96]
        else:
            kv[SEG[3] : SEG[4]] = pick(4, meta[OWN + 4 * b + 2], next_ref[0, 0:BLK])
        kv[SEG[4] : SEG[5]] = far_ref[0, 48 * b : 48 * b + 48]

    def products(b):
        kv, s, dp = kvs.at[b % 2], ss.at[b % 2], dps.at[b % 2]
        yield lambda: gather(b)

        def tile(lo, hi, which):
            if which:
                dp[lo:hi] = dot(kv[lo:hi, HD:], g_of(b), ((1,), (1,)))
            else:
                s[lo:hi] = dot(kv[lo:hi, :HD], q_of(b), ((1,), (1,)))

        for which in (0, 1):
            for lo, hi in ((0, BLK), (BLK, KEYS)):
                yield functools.partial(tile, lo, hi, which)

    def softmax(b):
        s, dp, p, ds = ss.at[b % 2], dps.at[b % 2], ps.at[b % 2], dss.at[b % 2]
        biases = [None] + [jnp.where(meta[4 * b + k] == 1, 0.0, NEG).astype(F32) for k in range(LEVELS)]
        row = lax.broadcasted_iota(jnp.int32, (128, 128), 0)
        col = lax.broadcasted_iota(jnp.int32, (128, 128), 1)
        upper = row <= col
        c = SCALE * LOG2E
        for i in range(3):
            lanes = slice(128 * i, 128 * i + 128)
            tiles = [(128 * j, 128 * j + 128, 0) for j in range(i + 1)]
            tiles += [(BLK + 128 * j, BLK + 128 * j + 128, 1) for j in range(3)]
            tiles += [(SEG[2], SEG[2] + 96, 2), (SEG[2] + 96, SEG[3], 2), (SEG[3], SEG[4], 3), (SEG[4], SEG[5], 4)]
            st = dict(m=None, total=None, delta=None)

            def top(lo, hi, seg, i=i, lanes=lanes, st=st):
                t = s[lo:hi, lanes]
                if seg == 0 and lo == 128 * i:
                    t = jnp.where(upper, t, NEG)
                t = jnp.max(t, axis=0, keepdims=True)
                if biases[seg] is not None:
                    t = t + biases[seg]
                st["m"] = t if st["m"] is None else jnp.maximum(st["m"], t)

            def exps(lo, hi, seg, i=i, lanes=lanes, st=st):
                m = st["m"] * c
                shift = m if biases[seg] is None else m - biases[seg]
                t = s[lo:hi, lanes] * c - shift
                if seg == 0 and lo == 128 * i:
                    t = jnp.where(upper, t, NEG)
                e = jnp.exp2(t)
                s[lo:hi, lanes] = e
                total = jnp.sum(e, axis=0, keepdims=True)
                delta = jnp.sum(e * dp[lo:hi, lanes], axis=0, keepdims=True)
                st["total"] = total if st["total"] is None else st["total"] + total
                st["delta"] = delta if st["delta"] is None else st["delta"] + delta

            def norm(st=st):
                st["inv"] = 1.0 / st["total"]
                st["delta"] = st["delta"] * st["inv"]

            def scores(lo, hi, lanes=lanes, st=st):
                prob = s[lo:hi, lanes] * st["inv"]
                p[lo:hi, lanes] = prob.astype(BF16)
                ds[lo:hi, lanes] = (prob * (dp[lo:hi, lanes] - st["delta"])).astype(BF16)

            for lo, hi, seg in tiles:
                yield functools.partial(top, lo, hi, seg)
            for lo, hi, seg in tiles:
                yield functools.partial(exps, lo, hi, seg)
            yield norm
            for lo, hi, seg in tiles:
                yield functools.partial(scores, lo, hi)

    def gradients(b):
        kv, p, ds = kvs.at[b % 2], ps.at[b % 2], dss.at[b % 2]

        def queries():
            dq_ref[0, b] = (dot(ds[...], kv[:, :HD], ((0,), (0,))) * SCALE).astype(BF16)

        def pair(lo, hi):
            dk = dot(ds[lo:hi], q_of(b), ((1,), (0,))) * SCALE
            dv = dot(p[lo:hi], g_of(b), ((1,), (0,)))
            return jnp.concatenate([dk, dv], axis=1)

        def own():
            acc_ref[0, b] = pair(0, BLK)

        def near():
            term = pair(BLK, 2 * BLK)
            if b == 0:
                prev[...] = term
            else:
                acc_ref[0, b - 1] += term

        def two():
            term = pair(SEG[2], SEG[3]).astype(BF16)
            if b == 0:
                rnext_ref[0, NEXT_L1:NEXT_L2] = term
            elif b == 1:
                prev[...] += spread(2, meta[OWN + 4 * b + 1], term)
            else:
                acc_ref[0, b - 2] += spread(2, meta[OWN + 4 * b + 1], term)

        def four():
            term = pair(SEG[3], SEG[4]).astype(BF16)
            if b < 3:
                rnext_ref[0, NEXT_L2 + 96 * b : NEXT_L2 + 96 * b + 96] = term
            else:
                rnext_ref[0, 0:BLK] = (prev[...] + spread(4, meta[OWN + 4 * b + 2], term)).astype(BF16)

        def eight():
            rfar_ref[0, 48 * b : 48 * b + 48] = pair(SEG[4], SEG[5]).astype(BF16)

        yield own
        yield near
        yield two
        yield four
        yield eight
        yield queries

    for i in range(2):
        ps[i, 0:BLK] = jnp.zeros((BLK, BLK), BF16)
        dss[i, 0:BLK] = jnp.zeros((BLK, BLK), BF16)
    emit(products(0))
    for b in range(GROUP):
        emit(softmax(b))
        if b + 1 < GROUP:
            emit(products(b + 1))
        emit(gradients(b))


def join_kernel(meta, acc_ref, dq_ref, near_ref, far_ref, z_ref):
    for b in range(GROUP):
        t = acc_ref[0, b] + spread(8, meta[AFT + 4 * b + 3], far_ref[0, 48 * b : 48 * b + 48])
        if b < 3:
            lo = NEXT_L2 + 96 * b
            t = t + spread(4, meta[NXT + 4 * b + 2], near_ref[0, lo : lo + 96])
        if b == 2:
            t = t + spread(2, meta[NXT + 1], near_ref[0, NEXT_L1:NEXT_L2])
        if b == 3:
            t = t + near_ref[0, 0:BLK].astype(F32)
        at = slice(2 * b, 2 * b + 2)
        z_ref[at, 0] = dq_ref[0, b].reshape(2, HALF, HD)
        z_ref[at, 1] = t[:, :HD].astype(BF16).reshape(2, HALF, HD)
        z_ref[at, 2] = t[:, HD:].astype(BF16).reshape(2, HALF, HD)


def columns(pair, device):
    return pl.ds((pair * LINE + device) * PAIR * HD, PAIR * HD)


def pack_kernel(pair, count, *refs):
    arrays, x_ref, (held, ins, sems) = refs[:count], refs[-4], refs[-3:]
    width = LINE * PAIR * HD
    reads = [
        pltpu.make_async_copy(a.at[:, pl.ds(pair * width, width)], held.at[i], ins.at[i])
        for i, a in enumerate(arrays)
    ]
    for read in reads:
        read.start()
    writes = []
    for i, read in enumerate(reads):
        read.wait()
        for g in range(LINE):
            write = pltpu.make_async_copy(held.at[i, :, columns(0, g)], x_ref.at[g, i], sems.at[i, g])
            write.start()
            writes.append(write)
    for write in writes:
        write.wait()


def unpack_kernel(pair, w_ref, *refs):
    outs, (held, ins, sems) = refs[-6:-3], refs[-3:]
    reads = [pltpu.make_async_copy(w_ref.at[g], held.at[g], ins.at[g]) for g in range(LINE)]
    for read in reads:
        read.start()
    writes = []
    for g, read in enumerate(reads):
        read.wait()
        for i in range(3):
            write = pltpu.make_async_copy(held.at[g, i], outs[i].at[:, columns(pair, g)], sems.at[g, i])
            write.start()
            writes.append(write)
    for write in writes:
        write.wait()


SMEM = pl.BlockSpec(memory_space=pltpu.SMEM)
ANY = pl.BlockSpec(memory_space=pl.ANY)


def params(mib, axes=1):
    return pltpu.CompilerParams(
        dimension_semantics=("arbitrary",) * axes, vmem_limit_bytes=mib * 2**20
    )


def whole(shape):
    return pl.BlockSpec(shape, lambda b: (0,) * len(shape))


def y_spec(head, arrays):
    return pl.BlockSpec((LINE, 1, arrays, HALF, HD), lambda b: (0, head, 0, 0, 0))


def cost(flops, size, exps=0):
    return pl.CostEstimate(flops=int(flops), bytes_accessed=int(size), transcendentals=int(exps))


NEAR = (PAIR, NEXT_ROWS, 2 * HD)
FAR = (PAIR, FAR_ROWS, 2 * HD)


def a_head(shape):
    return pl.BlockSpec((1, *shape[1:]), lambda h: (h,) + (0,) * (len(shape) - 1))


def lanes_of(arrays, first):
    return pl.BlockSpec((LINE, arrays, HALF, HD), lambda h: (0, first // arrays, 0, h))


def packed(arrays, pair, after=()):
    count = len(arrays)
    return pl.pallas_call(
        functools.partial(pack_kernel, pair, count),
        in_specs=[ANY] * (count + len(after)),
        out_specs=ANY,
        out_shape=jax.ShapeDtypeStruct((LINE, count, HALF, PAIR * HD), BF16),
        scratch_shapes=[
            pltpu.VMEM((count, HALF, LINE * PAIR * HD), BF16),
            pltpu.SemaphoreType.DMA((count,)),
            pltpu.SemaphoreType.DMA((count, LINE)),
        ],
        compiler_params=pltpu.CompilerParams(vmem_limit_bytes=60 * 2**20),
        cost_estimate=cost(0, 2**23),
        name="packed",
    )(*arrays, *after)


def unpacked(w, pair, into):
    into = tuple(into)
    return pl.pallas_call(
        functools.partial(unpack_kernel, pair),
        in_specs=[ANY] * (1 + len(into)),
        out_specs=[ANY] * 3,
        out_shape=[jax.ShapeDtypeStruct((HALF, 2 * LINE * PAIR * HD), BF16)] * 3,
        input_output_aliases={1 + i: i for i in range(len(into))},
        scratch_shapes=[
            pltpu.VMEM((LINE, 3, HALF, PAIR * HD), BF16),
            pltpu.SemaphoreType.DMA((LINE,)),
            pltpu.SemaphoreType.DMA((LINE, 3)),
        ],
        compiler_params=pltpu.CompilerParams(vmem_limit_bytes=8 * 2**20),
        cost_estimate=cost(0, 2**23),
        name="unpacked",
    )(w, *into)


def rows_to_send(meta, y):
    return pl.pallas_call(
        send_kernel,
        grid=(1,),
        in_specs=[SMEM, pl.BlockSpec((LINE, 2, HALF, PAIR * HD), lambda i: (0, 0, 0, 0))],
        out_specs=[whole(NEAR), whole(FAR)],
        out_shape=[jax.ShapeDtypeStruct(NEAR, BF16), jax.ShapeDtypeStruct(FAR, BF16)],
        compiler_params=params(32),
        cost_estimate=cost(2**28, 2**22),
        name="rows_to_send",
    )(meta, y)


def attention(meta, y, w, first, near, far, after=()):
    sums = (PAIR, GROUP, BLK, 2 * HD)
    queries = (PAIR, GROUP, BLK, HD)
    return pl.pallas_call(
        main_kernel,
        grid=(PAIR,),
        in_specs=[SMEM, lanes_of(2, 0), lanes_of(2, first), a_head(NEAR), a_head(FAR)] + [ANY] * len(after),
        out_specs=[a_head(queries), a_head(sums), a_head(NEAR), a_head(FAR)],
        out_shape=[
            jax.ShapeDtypeStruct(queries, BF16),
            jax.ShapeDtypeStruct(sums, F32),
            jax.ShapeDtypeStruct(NEAR, BF16),
            jax.ShapeDtypeStruct(FAR, BF16),
        ],
        scratch_shapes=[
            pltpu.VMEM((2, KEYS, 2 * HD), BF16),
            pltpu.VMEM((2, KEYS, BLK), F32),
            pltpu.VMEM((2, KEYS, BLK), F32),
            pltpu.VMEM((2, KEYS, BLK), BF16),
            pltpu.VMEM((2, KEYS, BLK), BF16),
            pltpu.VMEM((BLK, 2 * HD), F32),
        ],
        compiler_params=params(40),
        cost_estimate=cost(PAIR * GROUP * BLK * KEYS * HD * COST, 10 * 2**20, 0),
        name="attention",
    )(meta, y, w, near, far, *after)


def joined(meta, acc, dq, near, far, after=()):
    return pl.pallas_call(
        lambda *refs: join_kernel(*refs[:5], refs[-1]),
        grid=(PAIR,),
        in_specs=[SMEM, a_head(acc.shape), a_head(dq.shape), a_head(NEAR), a_head(FAR)] + [ANY] * len(after),
        out_specs=lanes_of(3, 0),
        out_shape=jax.ShapeDtypeStruct((LINE, 3, HALF, PAIR * HD), BF16),
        compiler_params=params(32),
        cost_estimate=cost(2**28, 2**22),
        name="joined",
    )(meta, acc, dq, near, far, *after)


def shift(value, steps):
    count = lax.axis_size(GROUP_AXES)
    pairs = [(i, i + steps) for i in range(count) if 0 <= i + steps < count]
    return lax.ppermute(value, GROUP_AXES, pairs)


def both(value, axis):
    other = lax.ppermute(value, axis, [(0, 1), (1, 0)])
    first = lax.axis_index(axis) == 0
    return jnp.stack([jnp.where(first, value, other), jnp.where(first, other, value)])


def rows_of(pattern, phase):
    own = jnp.concatenate([pattern, phase], axis=1)
    return jnp.concatenate([own, shift(own, -1), shift(own, -2)], axis=0)


def meta_of(rows):
    rows = both(both(rows, "core"), "yh").reshape(GROUP, 3, 2 * LEVELS)
    block = lax.axis_index(GROUP_AXES) * GROUP + jnp.arange(GROUP)
    distance = 2 ** jnp.arange(LEVELS)
    active = (rows[:, 0, :LEVELS] == 1) & (block[:, None] >= distance[None, :])
    phases = rows[:, :, LEVELS:].transpose(1, 0, 2)
    return jnp.concatenate([active.astype(jnp.int32).reshape(-1), phases.reshape(-1)])


def exchange(x):
    return lax.all_to_all(x, LINE_AXES, 0, 0, tiled=True)


def body(queries, keys, values, grad_out, pattern, phase):
    y0 = exchange(packed((keys, values, queries, grad_out), 0))
    rows = rows_of(pattern, phase)
    y1 = exchange(packed((keys, values), 1, (rows,)))
    meta = meta_of(rows)
    near0, far0 = rows_to_send(meta, y0)
    w1 = exchange(packed((queries, grad_out), 1, (near0,)))
    near1, far1 = rows_to_send(meta, y1)

    def grads(y, w, first, near, far, after=()):
        dq, acc, near, far = attention(meta, y, w, first, shift(near, 1), shift(far, 2), after)
        return acc, dq, shift(near, -1), shift(far, -2)

    g0 = grads(y0, y0, 2, near0, far0, (near1,))
    g1 = grads(y1, w1, 0, near1, far1, (g0[0],))
    z0 = joined(meta, *g0, (g1[0],))
    z1 = joined(meta, *g1, (z0,))
    out = unpacked(exchange(z0), 0, ())
    return tuple(unpacked(exchange(z1), 1, out))


def solution(mesh):
    sizes = (4, 4, 2, 2, 2)
    line = Mesh(mesh.devices.reshape(sizes), ("z", "x", "yh", "core", "yl"))
    ctx = ("z", "x", "yh", "core")
    tokens = P((*ctx, "yl"), None)
    return jax.shard_map(
        body,
        mesh=line,
        in_specs=(tokens,) * 4 + (P(ctx, None),) * 2,
        out_specs=(tokens,) * 3,
        check_vma=False,
    )
```

```python
import functools
import math

import jax
import jax.numpy as jnp
from jax import lax
from jax.experimental import pallas as pl
from jax.experimental.pallas import tpu as pltpu
from jax.sharding import Mesh, PartitionSpec as P

HD = 128
BLK = 384
HALF = 192
LEVELS = 4
LINE = 8
GROUP = 4
PAIR = 2
NEG = -1e30
COST = 30
SCALE = HD**-0.5
LOG2E = math.log2(math.e)
NEXT_L1 = BLK
NEXT_L2 = BLK + BLK // 2
NEXT_ROWS = NEXT_L2 + 3 * (BLK // 4)
FAR_ROWS = GROUP * (BLK // 8)
KEYS = BLK + BLK + BLK // 2 + BLK // 4 + BLK // 8
SEG = [0, BLK, 2 * BLK, 2 * BLK + BLK // 2, 2 * BLK + BLK // 2 + BLK // 4, KEYS]
OWN, NXT, AFT = 16, 32, 48
LINE_AXES = ("yh", "core", "yl")
GROUP_AXES = ("z", "x")
F32 = jnp.float32
BF16 = jnp.bfloat16


def dot(a, b, dims):
    return lax.dot_general(a, b, ((dims[0], dims[1]), ((), ())), preferred_element_type=F32)


def picker(stride, phase):
    rows = BLK // stride
    row = lax.broadcasted_iota(jnp.int32, (rows, BLK), 0)
    col = lax.broadcasted_iota(jnp.int32, (rows, BLK), 1)
    return jnp.where(col == row * stride + (phase & (stride - 1)), 1.0, 0.0).astype(BF16)


def spreader(stride, phase):
    cols = BLK // stride
    row = lax.broadcasted_iota(jnp.int32, (BLK, cols), 0)
    col = lax.broadcasted_iota(jnp.int32, (BLK, cols), 1)
    return jnp.where(row == col * stride + (phase & (stride - 1)), 1.0, 0.0).astype(BF16)


def pick(stride, phase, rows):
    return dot(picker(stride, phase), rows, ((1,), (0,))).astype(BF16)


def spread(stride, phase, rows):
    return dot(spreader(stride, phase), rows, ((1,), (0,)))


def kv_of(y_ref, block):
    at = slice(2 * block, 2 * block + 2)
    return jnp.concatenate([y_ref[at, 0].reshape(BLK, HD), y_ref[at, 1].reshape(BLK, HD)], axis=1)


def send_kernel(meta, y_ref, near_ref, far_ref):
    for h in range(PAIR):
        y = y_ref.at[:, :, :, h * HD : (h + 1) * HD]
        near_ref[h, 0:BLK] = kv_of(y, 3)
        near_ref[h, NEXT_L1:NEXT_L2] = pick(2, meta[NXT + 1], kv_of(y, 2))
        for b in range(3):
            lo = NEXT_L2 + b * 96
            near_ref[h, lo : lo + 96] = pick(4, meta[NXT + 4 * b + 2], kv_of(y, b))
        for b in range(GROUP):
            far_ref[h, 48 * b : 48 * b + 48] = pick(8, meta[AFT + 4 * b + 3], kv_of(y, b))


def emit(pieces):
    for piece in pieces:
        piece()


def main_kernel(meta, y_ref, w_ref, next_ref, far_ref, *refs):
    dq_ref, acc_ref, rnext_ref, rfar_ref, kvs, ss, dps, ps, dss, prev = refs[-10:]

    def q_of(b):
        return w_ref[2 * b : 2 * b + 2, 0].reshape(BLK, HD)

    def g_of(b):
        return w_ref[2 * b : 2 * b + 2, 1].reshape(BLK, HD)

    def gather(b):
        kv = kvs.at[b % 2]
        last = [None, lambda: next_ref[0, 0:BLK]] + [functools.partial(kv_of, y_ref, i) for i in range(b + 1)]
        own, one, two = last[b + 2], last[b + 1], last[b]
        kv[0:BLK] = own()
        kv[SEG[1] : SEG[2]] = one()
        if two is None:
            kv[SEG[2] : SEG[3]] = next_ref[0, NEXT_L1:NEXT_L2]
        else:
            kv[SEG[2] : SEG[3]] = pick(2, meta[OWN + 4 * b + 1], two())
        if b < 3:
            kv[SEG[3] : SEG[4]] = next_ref[0, NEXT_L2 + 96 * b : NEXT_L2 + 96 * b + 96]
        else:
            kv[SEG[3] : SEG[4]] = pick(4, meta[OWN + 4 * b + 2], next_ref[0, 0:BLK])
        kv[SEG[4] : SEG[5]] = far_ref[0, 48 * b : 48 * b + 48]

    def products(b):
        kv, s, dp = kvs.at[b % 2], ss.at[b % 2], dps.at[b % 2]
        yield lambda: gather(b)

        def tile(lo, hi, which):
            if which:
                dp[lo:hi] = dot(kv[lo:hi, HD:], g_of(b), ((1,), (1,)))
            else:
                s[lo:hi] = dot(kv[lo:hi, :HD], q_of(b), ((1,), (1,)))

        for which in (0, 1):
            for lo, hi in ((0, BLK), (BLK, KEYS)):
                yield functools.partial(tile, lo, hi, which)

    def softmax(b):
        s, dp, p, ds = ss.at[b % 2], dps.at[b % 2], ps.at[b % 2], dss.at[b % 2]
        biases = [None] + [jnp.where(meta[4 * b + k] == 1, 0.0, NEG).astype(F32) for k in range(LEVELS)]
        row = lax.broadcasted_iota(jnp.int32, (128, 128), 0)
        col = lax.broadcasted_iota(jnp.int32, (128, 128), 1)
        upper = row <= col
        c = SCALE * LOG2E
        for i in range(3):
            lanes = slice(128 * i, 128 * i + 128)
            tiles = [(128 * j, 128 * j + 128, 0) for j in range(i + 1)]
            tiles += [(BLK + 128 * j, BLK + 128 * j + 128, 1) for j in range(3)]
            tiles += [(SEG[2], SEG[2] + 96, 2), (SEG[2] + 96, SEG[3], 2), (SEG[3], SEG[4], 3), (SEG[4], SEG[5], 4)]
            st = dict(m=None, total=None, delta=None)

            def top(lo, hi, seg, i=i, lanes=lanes, st=st):
                t = s[lo:hi, lanes]
                if seg == 0 and lo == 128 * i:
                    t = jnp.where(upper, t, NEG)
                t = jnp.max(t, axis=0, keepdims=True)
                if biases[seg] is not None:
                    t = t + biases[seg]
                st["m"] = t if st["m"] is None else jnp.maximum(st["m"], t)

            def exps(lo, hi, seg, i=i, lanes=lanes, st=st):
                m = st["m"] * c
                shift = m if biases[seg] is None else m - biases[seg]
                t = s[lo:hi, lanes] * c - shift
                if seg == 0 and lo == 128 * i:
                    t = jnp.where(upper, t, NEG)
                e = jnp.exp2(t)
                s[lo:hi, lanes] = e
                total = jnp.sum(e, axis=0, keepdims=True)
                delta = jnp.sum(e * dp[lo:hi, lanes], axis=0, keepdims=True)
                st["total"] = total if st["total"] is None else st["total"] + total
                st["delta"] = delta if st["delta"] is None else st["delta"] + delta

            def norm(st=st):
                st["inv"] = 1.0 / st["total"]
                st["delta"] = st["delta"] * st["inv"]

            def scores(lo, hi, lanes=lanes, st=st):
                prob = s[lo:hi, lanes] * st["inv"]
                p[lo:hi, lanes] = prob.astype(BF16)
                ds[lo:hi, lanes] = (prob * (dp[lo:hi, lanes] - st["delta"])).astype(BF16)

            for lo, hi, seg in tiles:
                yield functools.partial(top, lo, hi, seg)
            for lo, hi, seg in tiles:
                yield functools.partial(exps, lo, hi, seg)
            yield norm
            for lo, hi, seg in tiles:
                yield functools.partial(scores, lo, hi)

    def gradients(b):
        kv, p, ds = kvs.at[b % 2], ps.at[b % 2], dss.at[b % 2]

        def queries():
            part = dot(ds[...], kv[:, :HD], ((0,), (0,))) * SCALE
            dq_ref[2 * b : 2 * b + 2] = part.astype(BF16).reshape(2, HALF, HD)

        def pair(lo, hi):
            dk = dot(ds[lo:hi], q_of(b), ((1,), (0,))) * SCALE
            dv = dot(p[lo:hi], g_of(b), ((1,), (0,)))
            return jnp.concatenate([dk, dv], axis=1)

        def own():
            acc_ref[0, b] = pair(0, BLK)

        def near():
            term = pair(BLK, 2 * BLK)
            if b == 0:
                prev[...] = term
            else:
                acc_ref[0, b - 1] += term

        def two():
            term = pair(SEG[2], SEG[3]).astype(BF16)
            if b == 0:
                rnext_ref[0, NEXT_L1:NEXT_L2] = term
            elif b == 1:
                prev[...] += spread(2, meta[OWN + 4 * b + 1], term)
            else:
                acc_ref[0, b - 2] += spread(2, meta[OWN + 4 * b + 1], term)

        def four():
            term = pair(SEG[3], SEG[4]).astype(BF16)
            if b < 3:
                rnext_ref[0, NEXT_L2 + 96 * b : NEXT_L2 + 96 * b + 96] = term
            else:
                rnext_ref[0, 0:BLK] = (prev[...] + spread(4, meta[OWN + 4 * b + 2], term)).astype(BF16)

        def eight():
            rfar_ref[0, 48 * b : 48 * b + 48] = pair(SEG[4], SEG[5]).astype(BF16)

        yield own
        yield near
        yield two
        yield four
        yield eight
        yield queries

    for i in range(2):
        ps[i, 0:BLK] = jnp.zeros((BLK, BLK), BF16)
        dss[i, 0:BLK] = jnp.zeros((BLK, BLK), BF16)
    emit(products(0))
    for b in range(GROUP):
        emit(softmax(b))
        if b + 1 < GROUP:
            emit(products(b + 1))
        emit(gradients(b))


def join_kernel(meta, acc_ref, near_ref, far_ref, *refs):
    z_ref = refs[-1]
    with_queries = z_ref.shape[1] == 3
    for b in range(GROUP):
        t = acc_ref[0, b] + spread(8, meta[AFT + 4 * b + 3], far_ref[0, 48 * b : 48 * b + 48])
        if b < 3:
            lo = NEXT_L2 + 96 * b
            t = t + spread(4, meta[NXT + 4 * b + 2], near_ref[0, lo : lo + 96])
        if b == 2:
            t = t + spread(2, meta[NXT + 1], near_ref[0, NEXT_L1:NEXT_L2])
        if b == 3:
            t = t + near_ref[0, 0:BLK].astype(F32)
        at = slice(2 * b, 2 * b + 2)
        if with_queries:
            z_ref[at, 0] = refs[0][at]
        z_ref[at, z_ref.shape[1] - 2] = t[:, :HD].astype(BF16).reshape(2, HALF, HD)
        z_ref[at, z_ref.shape[1] - 1] = t[:, HD:].astype(BF16).reshape(2, HALF, HD)


def columns(pair, device):
    return pl.ds((pair * LINE + device) * PAIR * HD, PAIR * HD)


def pack_kernel(pair, count, *refs):
    arrays, x_ref, (held, ins, sems) = refs[:count], refs[-4], refs[-3:]
    width = LINE * PAIR * HD
    reads = [
        pltpu.make_async_copy(a.at[:, pl.ds(pair * width, width)], held.at[i], ins.at[i])
        for i, a in enumerate(arrays)
    ]
    for read in reads:
        read.start()
    writes = []
    for i, read in enumerate(reads):
        read.wait()
        for g in range(LINE):
            write = pltpu.make_async_copy(held.at[i, :, columns(0, g)], x_ref.at[g, i], sems.at[i, g])
            write.start()
            writes.append(write)
    for write in writes:
        write.wait()


def unpack_kernel(pair, w_ref, *refs):
    (held, ins, sems), count = refs[-3:], w_ref.shape[1]
    outs = refs[-3 - count : -3]
    reads = [pltpu.make_async_copy(w_ref.at[g], held.at[g], ins.at[g]) for g in range(LINE)]
    for read in reads:
        read.start()
    writes = []
    for g, read in enumerate(reads):
        read.wait()
        for i in range(count):
            write = pltpu.make_async_copy(held.at[g, i], outs[i].at[:, columns(pair, g)], sems.at[g, i])
            write.start()
            writes.append(write)
    for write in writes:
        write.wait()


SMEM = pl.BlockSpec(memory_space=pltpu.SMEM)
ANY = pl.BlockSpec(memory_space=pl.ANY)


def params(mib, axes=1):
    return pltpu.CompilerParams(
        dimension_semantics=("arbitrary",) * axes, vmem_limit_bytes=mib * 2**20
    )


def whole(shape):
    return pl.BlockSpec(shape, lambda b: (0,) * len(shape))


def y_spec(head, arrays):
    return pl.BlockSpec((LINE, 1, arrays, HALF, HD), lambda b: (0, head, 0, 0, 0))


def cost(flops, size, exps=0):
    return pl.CostEstimate(flops=int(flops), bytes_accessed=int(size), transcendentals=int(exps))


NEAR = (PAIR, NEXT_ROWS, 2 * HD)
FAR = (PAIR, FAR_ROWS, 2 * HD)


def a_head(shape):
    return pl.BlockSpec((1, *shape[1:]), lambda h: (h,) + (0,) * (len(shape) - 1))


QUERY_GRADS = pl.BlockSpec((LINE, HALF, HD), lambda h: (0, 0, h))


def lanes_of(arrays, first):
    return pl.BlockSpec((LINE, arrays, HALF, HD), lambda h: (0, first // arrays, 0, h))


def packed(arrays, pair, after=()):
    count = len(arrays)
    return pl.pallas_call(
        functools.partial(pack_kernel, pair, count),
        in_specs=[ANY] * (count + len(after)),
        out_specs=ANY,
        out_shape=jax.ShapeDtypeStruct((LINE, count, HALF, PAIR * HD), BF16),
        scratch_shapes=[
            pltpu.VMEM((count, HALF, LINE * PAIR * HD), BF16),
            pltpu.SemaphoreType.DMA((count,)),
            pltpu.SemaphoreType.DMA((count, LINE)),
        ],
        compiler_params=pltpu.CompilerParams(vmem_limit_bytes=60 * 2**20),
        cost_estimate=cost(0, 2**23),
        name="packed",
    )(*arrays, *after)


def unpacked(w, pair, into=()):
    into, count = tuple(into), w.shape[1]
    return pl.pallas_call(
        functools.partial(unpack_kernel, pair),
        in_specs=[ANY] * (1 + len(into)),
        out_specs=[ANY] * count,
        out_shape=[jax.ShapeDtypeStruct((HALF, 2 * LINE * PAIR * HD), BF16)] * count,
        input_output_aliases={1 + i: i for i in range(len(into))},
        scratch_shapes=[
            pltpu.VMEM((LINE, count, HALF, PAIR * HD), BF16),
            pltpu.SemaphoreType.DMA((LINE,)),
            pltpu.SemaphoreType.DMA((LINE, count)),
        ],
        compiler_params=pltpu.CompilerParams(vmem_limit_bytes=8 * 2**20),
        cost_estimate=cost(0, 2**23),
        name="unpacked",
    )(w, *into)


def rows_to_send(meta, y):
    return pl.pallas_call(
        send_kernel,
        grid=(1,),
        in_specs=[SMEM, pl.BlockSpec((LINE, 2, HALF, PAIR * HD), lambda i: (0, 0, 0, 0))],
        out_specs=[whole(NEAR), whole(FAR)],
        out_shape=[jax.ShapeDtypeStruct(NEAR, BF16), jax.ShapeDtypeStruct(FAR, BF16)],
        compiler_params=params(32),
        cost_estimate=cost(2**28, 2**22),
        name="rows_to_send",
    )(meta, y)


def attention(meta, y, w, first, near, far, after=()):
    sums = (PAIR, GROUP, BLK, 2 * HD)
    return pl.pallas_call(
        main_kernel,
        grid=(PAIR,),
        in_specs=[SMEM, lanes_of(2, 0), lanes_of(2, first), a_head(NEAR), a_head(FAR)] + [ANY] * len(after),
        out_specs=[QUERY_GRADS, a_head(sums), a_head(NEAR), a_head(FAR)],
        out_shape=[
            pltpu.HBM((LINE, HALF, PAIR * HD), BF16),
            pltpu.HBM(sums, F32),
            pltpu.HBM(NEAR, BF16),
            pltpu.HBM(FAR, BF16),
        ],
        scratch_shapes=[
            pltpu.VMEM((2, KEYS, 2 * HD), BF16),
            pltpu.VMEM((2, KEYS, BLK), F32),
            pltpu.VMEM((2, KEYS, BLK), F32),
            pltpu.VMEM((2, KEYS, BLK), BF16),
            pltpu.VMEM((2, KEYS, BLK), BF16),
            pltpu.VMEM((BLK, 2 * HD), F32),
        ],
        compiler_params=params(60),
        cost_estimate=cost(PAIR * GROUP * BLK * KEYS * HD * COST, 10 * 2**20, 0),
        name="attention",
    )(meta, y, w, near, far, *after)


def joined(meta, acc, near, far, queries=(), after=()):
    arrays = 2 + len(queries)
    return pl.pallas_call(
        join_kernel,
        grid=(PAIR,),
        in_specs=[SMEM, a_head(acc.shape), a_head(NEAR), a_head(FAR)]
        + [QUERY_GRADS] * len(queries)
        + [ANY] * len(after),
        out_specs=lanes_of(arrays, 0),
        out_shape=pltpu.HBM((LINE, arrays, HALF, PAIR * HD), BF16),
        compiler_params=params(60),
        cost_estimate=cost(2**36, 2**22),
        name="joined",
    )(meta, acc, near, far, *queries, *after)


def shift(value, steps):
    count = lax.axis_size(GROUP_AXES)
    pairs = [(i, i + steps) for i in range(count) if 0 <= i + steps < count]
    return lax.ppermute(value, GROUP_AXES, pairs)


def both(value, axis):
    other = lax.ppermute(value, axis, [(0, 1), (1, 0)])
    first = lax.axis_index(axis) == 0
    return jnp.stack([jnp.where(first, value, other), jnp.where(first, other, value)])


def rows_of(pattern, phase):
    own = jnp.concatenate([pattern, phase], axis=1)
    return jnp.concatenate([own, shift(own, -1), shift(own, -2)], axis=0)


def meta_of(rows):
    rows = both(both(rows, "core"), "yh").reshape(GROUP, 3, 2 * LEVELS)
    block = lax.axis_index(GROUP_AXES) * GROUP + jnp.arange(GROUP)
    distance = 2 ** jnp.arange(LEVELS)
    active = (rows[:, 0, :LEVELS] == 1) & (block[:, None] >= distance[None, :])
    phases = rows[:, :, LEVELS:].transpose(1, 0, 2)
    return jnp.concatenate([active.astype(jnp.int32).reshape(-1), phases.reshape(-1)])


def exchange(x):
    return lax.all_to_all(x, LINE_AXES, 0, 0, tiled=True)


def body(queries, keys, values, grad_out, pattern, phase):
    y0 = exchange(packed((keys, values, queries, grad_out), 0))
    rows = rows_of(pattern, phase)
    y1 = exchange(packed((keys, values), 1, (rows,)))
    meta = meta_of(rows)
    near0, far0 = rows_to_send(meta, y0)
    w1 = exchange(packed((queries, grad_out), 1, (near0,)))
    near1, far1 = rows_to_send(meta, y1)

    def grads(y, w, first, near, far, after=()):
        dq, acc, near, far = attention(meta, y, w, first, shift(near, 1), shift(far, 2), after)
        return dq, (acc, shift(near, -1), shift(far, -2))

    dq0, g0 = grads(y0, y0, 2, near0, far0, (near1,))
    moved_q = exchange(dq0)
    dq1, g1 = grads(y1, w1, 0, near1, far1, (dq0,))
    z0 = joined(meta, *g0, (), (dq1, moved_q))
    z1 = joined(meta, *g1, (dq1,), (z0,))
    out_q = unpacked(moved_q[:, None], 0)
    out_kv = unpacked(exchange(z0), 0)
    return tuple(unpacked(exchange(z1), 1, (*out_q, *out_kv)))


def solution(mesh):
    sizes = (4, 4, 2, 2, 2)
    line = Mesh(mesh.devices.reshape(sizes), ("z", "x", "yh", "core", "yl"))
    ctx = ("z", "x", "yh", "core")
    tokens = P((*ctx, "yl"), None)
    return jax.shard_map(
        body,
        mesh=line,
        in_specs=(tokens,) * 4 + (P(ctx, None),) * 2,
        out_specs=(tokens,) * 3,
        check_vma=False,
    )
```

```python
import functools
import math

import jax
import jax.numpy as jnp
from jax import lax
from jax.experimental import pallas as pl
from jax.experimental.pallas import tpu as pltpu
from jax.sharding import Mesh, PartitionSpec as P

HD = 128
BLK = 384
HALF = 192
LEVELS = 4
LINE = 8
GROUP = 4
PAIR = 2
NEG = -1e30
COST = 30
SCALE = HD**-0.5
LOG2E = math.log2(math.e)
NEXT_L1 = BLK
NEXT_L2 = BLK + BLK // 2
NEXT_ROWS = NEXT_L2 + 3 * (BLK // 4)
FAR_ROWS = GROUP * (BLK // 8)
KEYS = BLK + BLK + BLK // 2 + BLK // 4 + BLK // 8
SEG = [0, BLK, 2 * BLK, 2 * BLK + BLK // 2, 2 * BLK + BLK // 2 + BLK // 4, KEYS]
OWN, NXT, AFT = 16, 32, 48
LINE_AXES = ("yh", "core", "yl")
GROUP_AXES = ("z", "x")
F32 = jnp.float32
BF16 = jnp.bfloat16


def dot(a, b, dims):
    return lax.dot_general(a, b, ((dims[0], dims[1]), ((), ())), preferred_element_type=F32)


def picker(stride, phase):
    rows = BLK // stride
    row = lax.broadcasted_iota(jnp.int32, (rows, BLK), 0)
    col = lax.broadcasted_iota(jnp.int32, (rows, BLK), 1)
    return jnp.where(col == row * stride + (phase & (stride - 1)), 1.0, 0.0).astype(BF16)


def spreader(stride, phase):
    cols = BLK // stride
    row = lax.broadcasted_iota(jnp.int32, (BLK, cols), 0)
    col = lax.broadcasted_iota(jnp.int32, (BLK, cols), 1)
    return jnp.where(row == col * stride + (phase & (stride - 1)), 1.0, 0.0).astype(BF16)


def pick(stride, phase, rows):
    return dot(picker(stride, phase), rows, ((1,), (0,))).astype(BF16)


def spread(stride, phase, rows):
    return dot(spreader(stride, phase), rows, ((1,), (0,)))


def kv_of(y_ref, block):
    at = slice(2 * block, 2 * block + 2)
    return jnp.concatenate([y_ref[at, 0].reshape(BLK, HD), y_ref[at, 1].reshape(BLK, HD)], axis=1)


def send_kernel(meta, y_ref, near_ref, far_ref):
    for h in range(PAIR):
        y = y_ref.at[:, :, :, h * HD : (h + 1) * HD]
        near_ref[h, 0:BLK] = kv_of(y, 3)
        near_ref[h, NEXT_L1:NEXT_L2] = pick(2, meta[NXT + 1], kv_of(y, 2))
        for b in range(3):
            lo = NEXT_L2 + b * 96
            near_ref[h, lo : lo + 96] = pick(4, meta[NXT + 4 * b + 2], kv_of(y, b))
        for b in range(GROUP):
            far_ref[h, 48 * b : 48 * b + 48] = pick(8, meta[AFT + 4 * b + 3], kv_of(y, b))


def emit(pieces):
    for piece in pieces:
        piece()


def main_kernel(meta, y_ref, w_ref, next_ref, far_ref, *refs):
    dq_ref, acc_ref, rnext_ref, rfar_ref, kvs, ss, dps, ps, dss, prev = refs[-10:]

    def q_of(b):
        return w_ref[2 * b : 2 * b + 2, 0].reshape(BLK, HD)

    def g_of(b):
        return w_ref[2 * b : 2 * b + 2, 1].reshape(BLK, HD)

    def gather(b):
        kv = kvs.at[b % 2]
        last = [None, lambda: next_ref[0, 0:BLK]] + [functools.partial(kv_of, y_ref, i) for i in range(b + 1)]
        own, one, two = last[b + 2], last[b + 1], last[b]
        kv[0:BLK] = own()
        kv[SEG[1] : SEG[2]] = one()
        if two is None:
            kv[SEG[2] : SEG[3]] = next_ref[0, NEXT_L1:NEXT_L2]
        else:
            kv[SEG[2] : SEG[3]] = pick(2, meta[OWN + 4 * b + 1], two())
        if b < 3:
            kv[SEG[3] : SEG[4]] = next_ref[0, NEXT_L2 + 96 * b : NEXT_L2 + 96 * b + 96]
        else:
            kv[SEG[3] : SEG[4]] = pick(4, meta[OWN + 4 * b + 2], next_ref[0, 0:BLK])
        kv[SEG[4] : SEG[5]] = far_ref[0, 48 * b : 48 * b + 48]

    def products(b):
        kv, s, dp = kvs.at[b % 2], ss.at[b % 2], dps.at[b % 2]
        yield lambda: gather(b)

        def tile(lo, hi, which):
            if which:
                dp[lo:hi] = dot(kv[lo:hi, HD:], g_of(b), ((1,), (1,)))
            else:
                s[lo:hi] = dot(kv[lo:hi, :HD], q_of(b), ((1,), (1,)))

        for which in (0, 1):
            yield functools.partial(tile, 0, KEYS, which)

    def softmax(b):
        s, dp, p, ds = ss.at[b % 2], dps.at[b % 2], ps.at[b % 2], dss.at[b % 2]
        biases = [None] + [jnp.where(meta[4 * b + k] == 1, 0.0, NEG).astype(F32) for k in range(LEVELS)]
        row = lax.broadcasted_iota(jnp.int32, (128, 128), 0)
        col = lax.broadcasted_iota(jnp.int32, (128, 128), 1)
        upper = row <= col
        c = SCALE * LOG2E
        for i in range(3):
            lanes = slice(128 * i, 128 * i + 128)
            tiles = [(128 * j, 128 * j + 128, 0) for j in range(i + 1)]
            tiles += [(BLK + 128 * j, BLK + 128 * j + 128, 1) for j in range(3)]
            tiles += [(SEG[2], SEG[2] + 96, 2), (SEG[2] + 96, SEG[3], 2), (SEG[3], SEG[4], 3), (SEG[4], SEG[5], 4)]
            st = dict(m=None, total=None, delta=None)

            def top(lo, hi, seg, i=i, lanes=lanes, st=st):
                t = s[lo:hi, lanes]
                if seg == 0 and lo == 128 * i:
                    t = jnp.where(upper, t, NEG)
                t = jnp.max(t, axis=0, keepdims=True)
                if biases[seg] is not None:
                    t = t + biases[seg]
                st["m"] = t if st["m"] is None else jnp.maximum(st["m"], t)

            def exps(lo, hi, seg, i=i, lanes=lanes, st=st):
                m = st["m"] * c
                shift = m if biases[seg] is None else m - biases[seg]
                t = s[lo:hi, lanes] * c - shift
                if seg == 0 and lo == 128 * i:
                    t = jnp.where(upper, t, NEG)
                e = jnp.exp2(t)
                s[lo:hi, lanes] = e
                total = jnp.sum(e, axis=0, keepdims=True)
                delta = jnp.sum(e * dp[lo:hi, lanes], axis=0, keepdims=True)
                st["total"] = total if st["total"] is None else st["total"] + total
                st["delta"] = delta if st["delta"] is None else st["delta"] + delta

            def norm(st=st):
                st["inv"] = 1.0 / st["total"]
                st["delta"] = st["delta"] * st["inv"]

            def scores(lo, hi, lanes=lanes, st=st):
                prob = s[lo:hi, lanes] * st["inv"]
                p[lo:hi, lanes] = prob.astype(BF16)
                ds[lo:hi, lanes] = (prob * (dp[lo:hi, lanes] - st["delta"])).astype(BF16)

            for lo, hi, seg in tiles:
                yield functools.partial(top, lo, hi, seg)
            for lo, hi, seg in tiles:
                yield functools.partial(exps, lo, hi, seg)
            yield norm
            for lo, hi, seg in tiles:
                yield functools.partial(scores, lo, hi)

    def gradients(b):
        kv, p, ds = kvs.at[b % 2], ps.at[b % 2], dss.at[b % 2]

        def queries():
            part = dot(ds[...], kv[:, :HD], ((0,), (0,))) * SCALE
            dq_ref[2 * b : 2 * b + 2] = part.astype(BF16).reshape(2, HALF, HD)

        def pair(lo, hi):
            dk = dot(ds[lo:hi], q_of(b), ((1,), (0,))) * SCALE
            dv = dot(p[lo:hi], g_of(b), ((1,), (0,)))
            return jnp.concatenate([dk, dv], axis=1)

        kept = []

        def thinned(lo, hi):
            if not kept:
                kept.append(pair(SEG[2], KEYS))
            return kept[0][lo - SEG[2] : hi - SEG[2]].astype(BF16)

        def own():
            acc_ref[0, b] = pair(0, BLK)

        def near():
            term = pair(BLK, 2 * BLK)
            if b == 0:
                prev[...] = term
            else:
                acc_ref[0, b - 1] += term

        def two():
            term = thinned(SEG[2], SEG[3])
            if b == 0:
                rnext_ref[0, NEXT_L1:NEXT_L2] = term
            elif b == 1:
                prev[...] += spread(2, meta[OWN + 4 * b + 1], term)
            else:
                acc_ref[0, b - 2] += spread(2, meta[OWN + 4 * b + 1], term)

        def four():
            term = thinned(SEG[3], SEG[4])
            if b < 3:
                rnext_ref[0, NEXT_L2 + 96 * b : NEXT_L2 + 96 * b + 96] = term
            else:
                rnext_ref[0, 0:BLK] = (prev[...] + spread(4, meta[OWN + 4 * b + 2], term)).astype(BF16)

        def eight():
            rfar_ref[0, 48 * b : 48 * b + 48] = thinned(SEG[4], SEG[5])

        yield own
        yield near
        yield two
        yield four
        yield eight
        yield queries

    for i in range(2):
        ps[i, 0:BLK] = jnp.zeros((BLK, BLK), BF16)
        dss[i, 0:BLK] = jnp.zeros((BLK, BLK), BF16)
    emit(products(0))
    for b in range(GROUP):
        emit(softmax(b))
        if b + 1 < GROUP:
            emit(products(b + 1))
        emit(gradients(b))


def join_kernel(meta, acc_ref, near_ref, far_ref, *refs):
    z_ref = refs[-1]
    with_queries = z_ref.shape[1] == 3
    for b in range(GROUP):
        t = acc_ref[0, b] + spread(8, meta[AFT + 4 * b + 3], far_ref[0, 48 * b : 48 * b + 48])
        if b < 3:
            lo = NEXT_L2 + 96 * b
            t = t + spread(4, meta[NXT + 4 * b + 2], near_ref[0, lo : lo + 96])
        if b == 2:
            t = t + spread(2, meta[NXT + 1], near_ref[0, NEXT_L1:NEXT_L2])
        if b == 3:
            t = t + near_ref[0, 0:BLK].astype(F32)
        at = slice(2 * b, 2 * b + 2)
        if with_queries:
            z_ref[at, 0] = refs[0][at]
        z_ref[at, z_ref.shape[1] - 2] = t[:, :HD].astype(BF16).reshape(2, HALF, HD)
        z_ref[at, z_ref.shape[1] - 1] = t[:, HD:].astype(BF16).reshape(2, HALF, HD)


def columns(pair, device):
    return pl.ds((pair * LINE + device) * PAIR * HD, PAIR * HD)


def pack_kernel(pair, count, *refs):
    arrays, x_ref, (held, ins, sems) = refs[:count], refs[-4], refs[-3:]
    width = LINE * PAIR * HD
    reads = [
        pltpu.make_async_copy(a.at[:, pl.ds(pair * width, width)], held.at[i], ins.at[i])
        for i, a in enumerate(arrays)
    ]
    for read in reads:
        read.start()
    writes = []
    for i, read in enumerate(reads):
        read.wait()
        for g in range(LINE):
            write = pltpu.make_async_copy(held.at[i, :, columns(0, g)], x_ref.at[g, i], sems.at[i, g])
            write.start()
            writes.append(write)
    for write in writes:
        write.wait()


def unpack_kernel(pair, w_ref, *refs):
    (held, ins, sems), count = refs[-3:], w_ref.shape[1]
    outs = refs[-3 - count : -3]
    reads = [pltpu.make_async_copy(w_ref.at[g], held.at[g], ins.at[g]) for g in range(LINE)]
    for read in reads:
        read.start()
    writes = []
    for g, read in enumerate(reads):
        read.wait()
        for i in range(count):
            write = pltpu.make_async_copy(held.at[g, i], outs[i].at[:, columns(pair, g)], sems.at[g, i])
            write.start()
            writes.append(write)
    for write in writes:
        write.wait()


SMEM = pl.BlockSpec(memory_space=pltpu.SMEM)
ANY = pl.BlockSpec(memory_space=pl.ANY)


def params(mib, axes=1):
    return pltpu.CompilerParams(
        dimension_semantics=("arbitrary",) * axes, vmem_limit_bytes=mib * 2**20
    )


def whole(shape):
    return pl.BlockSpec(shape, lambda b: (0,) * len(shape))


def y_spec(head, arrays):
    return pl.BlockSpec((LINE, 1, arrays, HALF, HD), lambda b: (0, head, 0, 0, 0))


def cost(flops, size, exps=0):
    return pl.CostEstimate(flops=int(flops), bytes_accessed=int(size), transcendentals=int(exps))


NEAR = (PAIR, NEXT_ROWS, 2 * HD)
FAR = (PAIR, FAR_ROWS, 2 * HD)


def a_head(shape):
    return pl.BlockSpec((1, *shape[1:]), lambda h: (h,) + (0,) * (len(shape) - 1))


QUERY_GRADS = pl.BlockSpec((LINE, HALF, HD), lambda h: (0, 0, h))


def lanes_of(arrays, first):
    return pl.BlockSpec((LINE, arrays, HALF, HD), lambda h: (0, first // arrays, 0, h))


def packed(arrays, pair, after=()):
    count = len(arrays)
    return pl.pallas_call(
        functools.partial(pack_kernel, pair, count),
        in_specs=[ANY] * (count + len(after)),
        out_specs=ANY,
        out_shape=jax.ShapeDtypeStruct((LINE, count, HALF, PAIR * HD), BF16),
        scratch_shapes=[
            pltpu.VMEM((count, HALF, LINE * PAIR * HD), BF16),
            pltpu.SemaphoreType.DMA((count,)),
            pltpu.SemaphoreType.DMA((count, LINE)),
        ],
        compiler_params=pltpu.CompilerParams(vmem_limit_bytes=60 * 2**20),
        cost_estimate=cost(0, 2**23),
        name="packed",
    )(*arrays, *after)


def unpacked(w, pair, into=()):
    into, count = tuple(into), w.shape[1]
    return pl.pallas_call(
        functools.partial(unpack_kernel, pair),
        in_specs=[ANY] * (1 + len(into)),
        out_specs=[ANY] * count,
        out_shape=[jax.ShapeDtypeStruct((HALF, 2 * LINE * PAIR * HD), BF16)] * count,
        input_output_aliases={1 + i: i for i in range(len(into))},
        scratch_shapes=[
            pltpu.VMEM((LINE, count, HALF, PAIR * HD), BF16),
            pltpu.SemaphoreType.DMA((LINE,)),
            pltpu.SemaphoreType.DMA((LINE, count)),
        ],
        compiler_params=pltpu.CompilerParams(vmem_limit_bytes=8 * 2**20),
        cost_estimate=cost(0, 2**23),
        name="unpacked",
    )(w, *into)


def rows_to_send(meta, y):
    return pl.pallas_call(
        send_kernel,
        grid=(1,),
        in_specs=[SMEM, pl.BlockSpec((LINE, 2, HALF, PAIR * HD), lambda i: (0, 0, 0, 0))],
        out_specs=[whole(NEAR), whole(FAR)],
        out_shape=[jax.ShapeDtypeStruct(NEAR, BF16), jax.ShapeDtypeStruct(FAR, BF16)],
        compiler_params=params(32),
        cost_estimate=cost(2**28, 2**22),
        name="rows_to_send",
    )(meta, y)


def attention(meta, y, w, first, near, far, after=()):
    sums = (PAIR, GROUP, BLK, 2 * HD)
    return pl.pallas_call(
        main_kernel,
        grid=(PAIR,),
        in_specs=[SMEM, lanes_of(2, 0), lanes_of(2, first), a_head(NEAR), a_head(FAR)] + [ANY] * len(after),
        out_specs=[QUERY_GRADS, a_head(sums), a_head(NEAR), a_head(FAR)],
        out_shape=[
            pltpu.HBM((LINE, HALF, PAIR * HD), BF16),
            pltpu.HBM(sums, F32),
            pltpu.HBM(NEAR, BF16),
            pltpu.HBM(FAR, BF16),
        ],
        scratch_shapes=[
            pltpu.VMEM((2, KEYS, 2 * HD), BF16),
            pltpu.VMEM((2, KEYS, BLK), F32),
            pltpu.VMEM((2, KEYS, BLK), F32),
            pltpu.VMEM((2, KEYS, BLK), BF16),
            pltpu.VMEM((2, KEYS, BLK), BF16),
            pltpu.VMEM((BLK, 2 * HD), F32),
        ],
        compiler_params=params(60),
        cost_estimate=cost(PAIR * GROUP * BLK * KEYS * HD * COST, 10 * 2**20, 0),
        name="attention",
    )(meta, y, w, near, far, *after)


def joined(meta, acc, near, far, queries=(), after=()):
    arrays = 2 + len(queries)
    return pl.pallas_call(
        join_kernel,
        grid=(PAIR,),
        in_specs=[SMEM, a_head(acc.shape), a_head(NEAR), a_head(FAR)]
        + [QUERY_GRADS] * len(queries)
        + [ANY] * len(after),
        out_specs=lanes_of(arrays, 0),
        out_shape=pltpu.HBM((LINE, arrays, HALF, PAIR * HD), BF16),
        compiler_params=params(60),
        cost_estimate=cost(2**36, 2**22),
        name="joined",
    )(meta, acc, near, far, *queries, *after)


def shift(value, steps):
    count = lax.axis_size(GROUP_AXES)
    pairs = [(i, i + steps) for i in range(count) if 0 <= i + steps < count]
    return lax.ppermute(value, GROUP_AXES, pairs)


def both(value, axis):
    other = lax.ppermute(value, axis, [(0, 1), (1, 0)])
    first = lax.axis_index(axis) == 0
    return jnp.stack([jnp.where(first, value, other), jnp.where(first, other, value)])


def rows_of(pattern, phase):
    own = jnp.concatenate([pattern, phase], axis=1)
    return jnp.concatenate([own, shift(own, -1), shift(own, -2)], axis=0)


def meta_of(rows):
    rows = both(both(rows, "core"), "yh").reshape(GROUP, 3, 2 * LEVELS)
    block = lax.axis_index(GROUP_AXES) * GROUP + jnp.arange(GROUP)
    distance = 2 ** jnp.arange(LEVELS)
    active = (rows[:, 0, :LEVELS] == 1) & (block[:, None] >= distance[None, :])
    phases = rows[:, :, LEVELS:].transpose(1, 0, 2)
    return jnp.concatenate([active.astype(jnp.int32).reshape(-1), phases.reshape(-1)])


def exchange(x):
    return lax.all_to_all(x, LINE_AXES, 0, 0, tiled=True)


def body(queries, keys, values, grad_out, pattern, phase):
    y0 = exchange(packed((keys, values, queries, grad_out), 0))
    rows = rows_of(pattern, phase)
    y1 = exchange(packed((keys, values), 1, (rows,)))
    meta = meta_of(rows)
    near0, far0 = rows_to_send(meta, y0)
    w1 = exchange(packed((queries, grad_out), 1, (near0,)))
    near1, far1 = rows_to_send(meta, y1)

    def grads(y, w, first, near, far, after=()):
        dq, acc, near, far = attention(meta, y, w, first, shift(near, 1), shift(far, 2), after)
        return dq, (acc, shift(near, -1), shift(far, -2))

    dq0, g0 = grads(y0, y0, 2, near0, far0, (near1,))
    moved_q = exchange(dq0)
    dq1, g1 = grads(y1, w1, 0, near1, far1, (dq0,))
    z0 = joined(meta, *g0, (), (dq1, moved_q))
    z1 = joined(meta, *g1, (dq1,), (z0,))
    out_q = unpacked(moved_q[:, None], 0)
    out_kv = unpacked(exchange(z0), 0)
    return tuple(unpacked(exchange(z1), 1, (*out_q, *out_kv)))


def solution(mesh):
    sizes = (4, 4, 2, 2, 2)
    line = Mesh(mesh.devices.reshape(sizes), ("z", "x", "yh", "core", "yl"))
    ctx = ("z", "x", "yh", "core")
    tokens = P((*ctx, "yl"), None)
    return jax.shard_map(
        body,
        mesh=line,
        in_specs=(tokens,) * 4 + (P(ctx, None),) * 2,
        out_specs=(tokens,) * 3,
        check_vma=False,
    )
```
